128 devices in a mesh: rep: 8 (over z, core), tp: 16 (over y, x).
Axes of the slice: x: 4, y: 4, z: 4, core: 2. Of those that a mesh axis runs over, the one named last changes fastest.
Arguments:
- queries: bfloat16 [2048, 64, 128], P(('rep', 'tp')), may hold values from -32 to 32
- cached_key_rows: bfloat16 [2048, 8, 256, 128], P(('rep', 'tp')), may hold values from -32 to 32
- cached_value_rows: bfloat16 [2048, 8, 256, 128], P(('rep', 'tp')), may hold values from -6 to 6
- fresh_key: bfloat16 [2048, 8, 128], P(('rep', 'tp')), may hold values from -6 to 6
- fresh_value: bfloat16 [2048, 8, 128], P(('rep', 'tp')), may hold values from -6 to 6
- lengths: int32 [2048], P(('rep', 'tp')), may hold values from 2 to 256
- adapter_index: int32 [2048, 1], P('rep'), may hold values from 0 to 127; in each aligned block of 256 rows (0 to 255, 256 to 511, ...) at most 4 rows name the same one
- skip_stream: bfloat16 [2048, 8192], P(('rep', 'tp')), may hold values from -2 to 2
- output_weight: bfloat16 [8192, 8192], P('tp'), may hold values from -0.0625 to 0.0625
- adapter_down_weight: bfloat16 [128, 8192, 64], P('rep', 'tp'), may hold values from -0.0625 to 0.0625
- adapter_up_weight: bfloat16 [128, 64, 8192], P('rep', None, 'tp'), may hold values from -0.75 to 0.75
Outputs:
- stream_updated: bfloat16 [2048, 8192], P(('rep', 'tp'))
The draws below stay inside these ranges and needn't reach their ends.
Inputs may be any that keep to these rules, and one draw needn't show every extreme that they name: `adapter_index`: among the 256 requests of each rep index, at most 4 name one adapter; every adapter is named by some request.
All inputs are finite; a program needn't handle non-finite values.
Results may differ from the reference program's by a relative error of at most 0.01.
Values may be sent and summed in bfloat16 or wider, within the bound.
No kernel may reach another device: no remote copies, remote signals or barrier semaphores. Data moves between devices by JAX's collectives and lax.ppermute only.
A program may use at most 128 MiB of HBM per device.

```python
import math
import jax
import jax.numpy as jnp
import numpy as np
from jax import lax

H = 64
KVH = 8
DH = 128
ADAPTER_RANK = 64
LOCAL_QUERIES = 16
KV_LEN = 256
HIDDEN_SIZE = 8192
ADAPTER_TOTAL = 128
REQ_REP = 256
GLOBAL_QUERIES = 2048
CAP = 4


def draw_queries(key, part):
    own_key = jax.random.fold_in(key, 11)
    values = jnp.clip(jax.random.normal(own_key, (GLOBAL_QUERIES, H, DH), jnp.float32), -6.0, 6.0)
    return values.astype(jnp.bfloat16)


def draw_cached_key_rows(key, part):
    own_key = jax.random.fold_in(key, 12)
    values = jnp.clip(jax.random.normal(own_key, (GLOBAL_QUERIES, KVH, KV_LEN, DH), jnp.float32), -6.0, 6.0)
    return values.astype(jnp.bfloat16)


def plant(entries, key, low, high):
    shape = entries.shape
    spot = [jax.random.randint(jax.random.fold_in(key, axis), (), 0, shape[axis]) for axis in range(len(shape))]
    entries = entries.at[tuple(spot)].set(low)
    longest = shape.index(max(shape))
    spot[longest] = (spot[longest] + 1) % shape[longest]
    return entries.at[tuple(spot)].set(high)


def block_levels(key, extent, cuts, low, largest):
    loudness, own = 1.0, jax.random.fold_in(key, 6)
    for dim, shards_of in cuts:
        draws = jnp.exp(jax.random.uniform(jax.random.fold_in(own, dim), (shards_of,), jnp.float32, low / len(cuts), largest / len(cuts)))
        loudness = loudness * jnp.repeat(draws, extent[dim] // shards_of).reshape([-1 if axis == dim else 1 for axis in range(len(extent))])
    return loudness


def deal_out(rng, own, number, rows, count, top, most, skew):
    sequence = jax.random.permutation(rng, count)
    crowded, usual = shares(count, rows * top, most, skew, True), shares(count, rows * top, most, skew, False)
    places = jnp.arange(count)

    def named(tallies, offset_by):
        used = int((tallies > 0).sum())
        fixed = max(1, used // 4)
        shifted = fixed + (places - fixed + offset_by * (used - fixed)) % max(1, count - fixed)
        return jnp.zeros((count,), jnp.int32).at[sequence[jnp.where(places < fixed, places, shifted)]].set(jnp.asarray(tallies, jnp.int32))

    tallies = jnp.where(number % 4 == 0, named(crowded, number // 4), named(usual, number - number // 4 - 1))
    mixed = jax.random.permutation(jax.random.fold_in(own, 3), count)
    giver, receiver = mixed[0:count // 2 * 2:2], mixed[1:count // 2 * 2:2]
    room = jnp.minimum(tallies[giver] - 1, most - tallies[receiver]) // 2
    room = jnp.where((giver == sequence[0]) | (receiver == sequence[0]) | (tallies[receiver] == 0), 0, jnp.maximum(room, 0))
    shifted = jax.random.randint(jax.random.fold_in(own, 4), (count // 2,), 0, 1 << 20) % (room + 1)
    tallies = tallies.at[giver].add(-shifted).at[receiver].add(shifted)
    labels = jnp.searchsorted(jnp.cumsum(tallies), jnp.arange(rows * top), side="right").astype(jnp.int32)
    listing = labels.reshape(top, rows).T
    listing = listing[jax.random.permutation(jax.random.fold_in(own, 1), rows)]
    offset_by = jax.random.randint(jax.random.fold_in(own, 2), (rows, 1), 0, top)
    return jnp.take_along_axis(listing, (jnp.arange(top)[None, :] + offset_by) % top, axis=1)


def shares(number_of, total, limit, slope, full):
    portions = [(1 << 20) // math.isqrt(rank ** slope) + 1 for rank in range(1, number_of + 1)]
    largest = limit if full else min(limit, max(-(-total // number_of), total * portions[0] // sum(portions)))
    least = 1 if total - largest >= number_of - 1 else 0
    given, rest = [largest] + [least] * (number_of - 1), total - largest - least * (number_of - 1)
    while rest > 0:
        movable = [i for i in range(1, number_of) if given[i] < largest] or [i for i in range(1, number_of) if given[i] < limit]
        pool, budget = sum([portions[i] for i in movable]), rest
        for i in movable:
            addition = min(limit - given[i], max(1, budget * portions[i] // pool), rest)
            given[i] = given[i] + addition
            rest = rest - addition
    return np.array(given)


def scatter_about(key, extent, deviation, most, cuts=(), kind=jnp.bfloat16):
    loudness = block_levels(key, extent, cuts, -0.22, 0.18) if cuts else 1.0
    result = jax.random.normal(key, extent, jnp.float32) * deviation * loudness
    return jnp.minimum(jnp.maximum(result, -most), most).astype(kind)


def setup_inputs(seed: int = 0) -> dict:
    arg_keys = jax.random.split(jax.random.key(seed), 12)
    queries = draw_queries(jax.random.fold_in(arg_keys[11], 71), 0)
    cached_key_rows = draw_cached_key_rows(jax.random.fold_in(arg_keys[11], 71), 0)
    cached_value_rows = scatter_about(arg_keys[2], (GLOBAL_QUERIES, KVH, KV_LEN, DH), 1.0, 6.0, ((0, 128),))
    fresh_key = scatter_about(arg_keys[3], (GLOBAL_QUERIES, KVH, DH), 1.0, 6.0, ((0, 128),))
    fresh_value = scatter_about(arg_keys[4], (GLOBAL_QUERIES, KVH, DH), 1.0, 6.0, ((0, 128),))
    lengths = plant(jax.random.randint(arg_keys[5], (GLOBAL_QUERIES,), 2, KV_LEN + 1), jax.random.fold_in(arg_keys[5], 1), 2, KV_LEN).astype(jnp.int32)
    adapter_index_keys = jax.random.split(jax.random.fold_in(arg_keys[6], 1), GLOBAL_QUERIES // REQ_REP)
    adapter_index_turns = jax.random.permutation(jax.random.fold_in(arg_keys[6], 3), GLOBAL_QUERIES // REQ_REP)
    adapter_index = jax.vmap(lambda own, number: deal_out(jax.random.fold_in(arg_keys[6], 2), own, number, REQ_REP, ADAPTER_TOTAL, 1, CAP, 2))(adapter_index_keys, adapter_index_turns).reshape((GLOBAL_QUERIES, 1))
    skip_stream = scatter_about(arg_keys[7], (GLOBAL_QUERIES, HIDDEN_SIZE), 0.3, 2.0, ((0, 128),))
    output_weight = scatter_about(arg_keys[8], (HIDDEN_SIZE, HIDDEN_SIZE), HIDDEN_SIZE ** -0.5, 0.0625, ((0, 16),))
    adapter_down_weight = scatter_about(arg_keys[9], (ADAPTER_TOTAL, HIDDEN_SIZE, ADAPTER_RANK), HIDDEN_SIZE ** -0.5, 0.0625, ((0, 8), (1, 16)))
    adapter_up_weight = scatter_about(arg_keys[10], (ADAPTER_TOTAL, ADAPTER_RANK, HIDDEN_SIZE), ADAPTER_RANK ** -0.5, 0.75, ((0, 8), (2, 16)))
    return {"queries": queries, "cached_key_rows": cached_key_rows, "cached_value_rows": cached_value_rows, "fresh_key": fresh_key, "fresh_value": fresh_value, "lengths": lengths, "adapter_index": adapter_index, "skip_stream": skip_stream, "output_weight": output_weight, "adapter_down_weight": adapter_down_weight, "adapter_up_weight": adapter_up_weight}


def attend_block(queries, cached_key_rows, cached_value_rows, fresh_key, fresh_value, lengths):
    count = queries.shape[0]
    grouped = queries.astype(jnp.float32).reshape(count, KVH, H // KVH, DH)
    factor = 1.0 / math.sqrt(DH)
    scores = jnp.einsum('rgqd,rgld->rgql', grouped, cached_key_rows.astype(jnp.float32)) * factor
    own = jnp.einsum('rgqd,rgd->rgq', grouped, fresh_key.astype(jnp.float32)) * factor
    position = jnp.arange(KV_LEN, dtype=jnp.int32)
    valid = position[None, None, None, :] < lengths[:, None, None, None]
    masked = jnp.where(valid, scores, -jnp.inf)
    top = jnp.maximum(lax.optimization_barrier(jnp.max(masked, axis=-1)), own)
    expo = jnp.where(valid, jnp.exp(scores - top[..., None]), 0.0)
    expo_own = jnp.exp(own - top)
    total = lax.optimization_barrier(jnp.sum(expo, axis=-1)) + expo_own
    probs = (expo / total[..., None]).astype(jnp.bfloat16)
    probs_own = (expo_own / total).astype(jnp.bfloat16)
    mixed = jnp.einsum('rgql,rgld->rgqd', probs.astype(jnp.float32), cached_value_rows.astype(jnp.float32))
    mixed = mixed + probs_own.astype(jnp.float32)[..., None] * fresh_value.astype(jnp.float32)[:, :, None, :]
    return mixed.reshape(count, HIDDEN_SIZE).astype(jnp.bfloat16)

def reference(queries, cached_key_rows, cached_value_rows, fresh_key, fresh_value, lengths, adapter_index, skip_stream, output_weight, adapter_down_weight, adapter_up_weight):
    lowrank_pairs = GLOBAL_QUERIES // LOCAL_QUERIES

    def attend_one(piece_list):
        return attend_block(*piece_list)
    mixed_heads = lax.map(attend_one, (queries.reshape(lowrank_pairs, LOCAL_QUERIES, H, DH), cached_key_rows.reshape(lowrank_pairs, LOCAL_QUERIES, KVH, KV_LEN, DH), cached_value_rows.reshape(lowrank_pairs, LOCAL_QUERIES, KVH, KV_LEN, DH), fresh_key.reshape(lowrank_pairs, LOCAL_QUERIES, KVH, DH), fresh_value.reshape(lowrank_pairs, LOCAL_QUERIES, KVH, DH), lengths.reshape(lowrank_pairs, LOCAL_QUERIES))).reshape(GLOBAL_QUERIES, HIDDEN_SIZE)
    dense_product = jnp.dot(mixed_heads, output_weight, preferred_element_type=jnp.float32)

    def lowrank_pair(piece_list):
        rows, selected_rows = piece_list
        down_matrix = adapter_down_weight[selected_rows].astype(jnp.float32)
        reduced_rows = jnp.einsum('rf,rfk->rk', rows.astype(jnp.float32), down_matrix).astype(jnp.bfloat16)
        up_matrix = adapter_up_weight[selected_rows].astype(jnp.float32)
        return jnp.einsum('rk,rkf->rf', reduced_rows.astype(jnp.float32), up_matrix).astype(jnp.bfloat16)
    chosen_position = adapter_index[:, 0].astype(jnp.int32)
    lowrank_delta = lax.map(lowrank_pair, (mixed_heads.reshape(lowrank_pairs, LOCAL_QUERIES, HIDDEN_SIZE), chosen_position.reshape(lowrank_pairs, LOCAL_QUERIES))).reshape(GLOBAL_QUERIES, HIDDEN_SIZE)
    stream_updated = skip_stream.astype(jnp.float32) + dense_product + 2.0 * lowrank_delta.astype(jnp.float32)
    return stream_updated.astype(jnp.bfloat16)
```

```python
import math

import jax
import jax.numpy as jnp
import numpy as np
from jax import lax
from jax.experimental import pallas as pl
from jax.experimental.pallas import tpu as pltpu
from jax.sharding import PartitionSpec as P

F32 = jnp.float32
BF16 = jnp.bfloat16
BOTH = ("rep", "tp")
SIDE = 4
VMEM_BYTES = 40 * 1024 * 1024


def place(z, c, y, x):
    return ((z * 2 + c) * SIDE + y) * SIDE + x


PLACES = [
    (z, c, y, x) for z in range(SIDE) for c in range(2) for y in range(SIDE) for x in range(SIDE)
]


def pass_plane(value, axis_of_core, offset):
    pairs = []
    for z, c, y, x in PLACES:
        if axis_of_core[c] == "x":
            to = place(z, c, y, (x + offset) % SIDE)
        else:
            to = place(z, c, (y + offset) % SIDE, x)
        pairs.append((place(z, c, y, x), to))
    return lax.ppermute(value, BOTH, pairs)


def pass_z(value, offset):
    pairs = [(place(z, c, y, x), place((z + offset) % SIDE, c, y, x)) for z, c, y, x in PLACES]
    return lax.ppermute(value, BOTH, pairs)


def pass_core(value):
    return lax.ppermute(
        value, BOTH, [(place(z, c, y, x), place(z, 1 - c, y, x)) for z, c, y, x in PLACES]
    )


def row_order():
    table = np.zeros((len(PLACES), SIDE * SIDE), np.int32)
    for z, c, y, x in PLACES:
        for first in range(SIDE):
            for second in range(SIDE):
                dx, dy = (first, second) if c == 0 else (second, first)
                table[place(z, c, y, x), first * SIDE + second] = (
                    (y + dy) % SIDE * SIDE + (x + dx) % SIDE
                )
    return table


PER_STEP = 2


def attend_kernel(
    lengths_ref, q_ref, k_ref, v_ref, fk_ref, fv_ref, o_ref, mixed_ref, *, groups, fold, span
):
    step = pl.program_id(0)
    heads = groups * fold
    width = q_ref.shape[-1]
    factor = 1.0 / math.sqrt(width)
    position = lax.broadcasted_iota(jnp.int32, (heads, span), 1)
    nt = (((1,), (1,)), ((), ()))
    for item in range(PER_STEP):
        row = step * PER_STEP + item
        q = q_ref[item]
        parts = []
        for g in range(groups):
            two = q[(g // 2) * 2 * fold : (g // 2 + 1) * 2 * fold]
            got = lax.dot_general(two, k_ref[item, g], nt, preferred_element_type=F32)
            parts.append(got[(g % 2) * fold : (g % 2 + 1) * fold])
        scores = jnp.concatenate(parts, axis=0) * factor
        fresh_k = jnp.broadcast_to(
            fk_ref[item].astype(F32)[:, None, :], (groups, fold, width)
        ).reshape(heads, width)
        own = jnp.sum(q.astype(F32) * fresh_k, axis=-1, keepdims=True) * factor
        valid = position < lengths_ref[row]
        masked = jnp.where(valid, scores, -jnp.inf)
        top = jnp.maximum(jnp.max(masked, axis=-1, keepdims=True), own)
        expo = jnp.exp(masked - top)
        expo_own = jnp.exp(own - top)
        total = jnp.sum(expo, axis=-1, keepdims=True) + expo_own
        inverse = 1.0 / total
        probs = (expo * inverse).astype(BF16)
        probs_own = (expo_own * inverse).astype(BF16).astype(F32)
        parts = []
        for g in range(groups):
            two = probs[(g // 2) * 2 * fold : (g // 2 + 1) * 2 * fold]
            got = jnp.dot(two, v_ref[item, g], preferred_element_type=F32)
            parts.append(got[(g % 2) * fold : (g % 2 + 1) * fold])
        fresh_v = jnp.broadcast_to(
            fv_ref[item].astype(F32)[:, None, :], (groups, fold, width)
        ).reshape(heads, width)
        mixed = jnp.concatenate(parts, axis=0) + probs_own * fresh_v
        mixed_ref[pl.ds(pl.multiple_of(row * heads, heads), heads), :] = mixed

    @pl.when(step == pl.num_programs(0) - 1)
    def _():
        blocks, rows, cols = o_ref.shape
        per_block = cols // width
        for h in range(heads):
            tile = jnp.concatenate(
                [
                    mixed_ref[pl.ds(half * 8 * heads + h, 8, stride=heads), :]
                    for half in range(rows // 8)
                ],
                axis=0,
            )
            lane = (h % per_block) * width
            o_ref[h // per_block, :, lane : lane + width] = tile.astype(BF16)


def attend(queries, keys, values, fresh_key, fresh_value, lengths, blocks):
    rows, heads, width = queries.shape
    groups, span = keys.shape[1], keys.shape[2]
    body = lambda *refs: attend_kernel(*refs, groups=groups, fold=heads // groups, span=span)
    cols = heads * width // blocks
    return pl.pallas_call(
        body,
        name="attend",
        out_shape=jax.ShapeDtypeStruct((blocks, rows, cols), BF16),
        grid_spec=pltpu.PrefetchScalarGridSpec(
            num_scalar_prefetch=1,
            grid=(rows // PER_STEP,),
            in_specs=[
                pl.BlockSpec((PER_STEP, heads, width), lambda i, _: (i, 0, 0)),
                pl.BlockSpec((PER_STEP, groups, span, width), lambda i, _: (i, 0, 0, 0)),
                pl.BlockSpec((PER_STEP, groups, span, width), lambda i, _: (i, 0, 0, 0)),
                pl.BlockSpec((PER_STEP, groups, width), lambda i, _: (i, 0, 0)),
                pl.BlockSpec((PER_STEP, groups, width), lambda i, _: (i, 0, 0)),
            ],
            out_specs=pl.BlockSpec((blocks, rows, cols), lambda i, _: (0, 0, 0)),
            scratch_shapes=[pltpu.VMEM((rows * heads, width), F32)],
        ),
        compiler_params=pltpu.CompilerParams(vmem_limit_bytes=VMEM_BYTES),
        cost_estimate=pl.CostEstimate(
            flops=4 * rows * heads * span * width,
            bytes_accessed=4 * rows * groups * span * width,
            transcendentals=rows * heads * span,
        ),
    )(lengths, queries, keys, values, fresh_key, fresh_value)


def whole(count):
    return [pl.BlockSpec(memory_space=pltpu.VMEM)] * count


def project_kernel(order_ref, f_ref, w_ref, *refs):
    outs, rows_ref = refs[:SIDE], refs[SIDE]
    block = f_ref.shape[1]

    @pl.when(pl.program_id(0) == 0)
    def _():
        for k in range(SIDE * SIDE):
            rows_ref[k * block : (k + 1) * block, :] = f_ref[order_ref[k]]

    product = jnp.dot(rows_ref[...], w_ref[...], preferred_element_type=F32).astype(BF16)
    chunk = product.shape[0] // SIDE
    for k in range(SIDE):
        outs[k][...] = product[k * chunk : (k + 1) * chunk]


def project(order, features, weight):
    blocks, rows, depth = features.shape
    cols = weight.shape[1]
    tile = 1024
    chunk = blocks * rows // SIDE
    return pl.pallas_call(
        project_kernel,
        name="project",
        out_shape=[jax.ShapeDtypeStruct((chunk, cols), BF16)] * SIDE,
        grid_spec=pltpu.PrefetchScalarGridSpec(
            num_scalar_prefetch=1,
            grid=(cols // tile,),
            in_specs=[
                pl.BlockSpec((blocks, rows, depth), lambda i, _: (0, 0, 0)),
                pl.BlockSpec((depth, tile), lambda i, _: (0, i)),
            ],
            out_specs=[pl.BlockSpec((chunk, tile), lambda i, _: (0, i))] * SIDE,
            scratch_shapes=[pltpu.VMEM((blocks * rows, depth), BF16)],
        ),
        compiler_params=pltpu.CompilerParams(vmem_limit_bytes=VMEM_BYTES),
        cost_estimate=pl.CostEstimate(
            flops=2 * blocks * rows * depth * cols,
            bytes_accessed=2 * depth * cols + 2 * blocks * rows * cols,
            transcendentals=0,
        ),
    )(order, features, weight)


def dispatch_kernel(slot_ref, f_ref, *outs):
    count = outs[0].shape[0]
    rows = f_ref.shape[0]
    features = f_ref[...]
    for k in range(SIDE):
        slots = lax.broadcasted_iota(jnp.int32, (count, rows), 0) + k * count
        placing = (slots == slot_ref[...]).astype(F32).astype(BF16)
        outs[k][...] = jnp.dot(placing, features, preferred_element_type=F32).astype(BF16)


def dispatch(slot, features, count):
    rows, depth = features.shape
    return pl.pallas_call(
        dispatch_kernel,
        name="dispatch",
        out_shape=[jax.ShapeDtypeStruct((count, depth), BF16)] * SIDE,
        in_specs=whole(2),
        out_specs=whole(SIDE),
        compiler_params=pltpu.CompilerParams(vmem_limit_bytes=VMEM_BYTES),
        cost_estimate=pl.CostEstimate(
            flops=2 * SIDE * count * rows * depth,
            bytes_accessed=2 * (rows + SIDE * count) * depth,
            transcendentals=0,
        ),
    )(slot.reshape(1, rows), features)


QUAD = 4


def lanes_of(rows, rank, swapped):
    row = lax.broadcasted_iota(jnp.int32, (rows, 2 * rank), 0)
    lane = lax.broadcasted_iota(jnp.int32, (rows, 2 * rank), 1)
    member = (row % 16) // QUAD
    half = (lane // rank) ^ swapped
    return (member % 2) == half, member < 2


def shrink_kernel(s0, s1, s2, s3, own_ref, other_ref, o_ref):
    rank = o_ref.shape[1] // 2
    nt = (((1,), (1,)), ((), ()))
    quads = own_ref.shape[0] // (QUAD * rank)
    for pair in range(quads):
        total = None
        for swapped, weight_ref in ((0, own_ref), (1, other_ref)):
            quad = pair + swapped * quads
            rows = jnp.concatenate([s[quad * 16 : (quad + 1) * 16, :] for s in (s0, s1, s2, s3)])
            weight = weight_ref[pair * QUAD * rank : (pair + 1) * QUAD * rank, :]
            if swapped:
                weight = jnp.concatenate(
                    [weight[(m ^ 1) * rank : ((m ^ 1) + 1) * rank] for m in range(QUAD)]
                )
            got = lax.dot_general(rows, weight, nt, preferred_element_type=F32)
            mine, first = lanes_of(rows.shape[0], rank, swapped)
            kept = jnp.where(first, got[:, : 2 * rank], got[:, 2 * rank :])
            kept = jnp.where(mine, kept, 0.0)
            total = kept if total is None else total + kept
        o_ref[pair * 64 : (pair + 1) * 64, :] = total.astype(BF16)


def shrink(slots, own, other):
    rank = 64
    return pl.pallas_call(
        shrink_kernel,
        name="shrink",
        out_shape=jax.ShapeDtypeStruct((own.shape[0] // (QUAD * rank) * 64, 2 * rank), BF16),
        in_specs=whole(6),
        out_specs=whole(1)[0],
        compiler_params=pltpu.CompilerParams(vmem_limit_bytes=VMEM_BYTES),
        cost_estimate=pl.CostEstimate(flops=2**28, bytes_accessed=2**22, transcendentals=0),
    )(*slots, own, other)


def grow_kernel(h_ref, own_ref, other_ref, *outs):
    rank = h_ref.shape[1] // 2
    quads = own_ref.shape[0] // (QUAD * rank)
    for pair in range(quads):
        held = h_ref[pair * 64 : (pair + 1) * 64, :].astype(F32)
        for swapped, weight_ref in ((0, own_ref), (1, other_ref)):
            quad = pair + swapped * quads
            weight = weight_ref[pair * QUAD * rank : (pair + 1) * QUAD * rank, :]
            if swapped:
                weight = jnp.concatenate(
                    [weight[(m ^ 1) * rank : ((m ^ 1) + 1) * rank] for m in range(QUAD)]
                )
            mine, first = lanes_of(held.shape[0], rank, swapped)
            left = jnp.where(mine & first, held, 0.0).astype(BF16)
            right = jnp.where(mine & ~first, held, 0.0).astype(BF16)
            got = jnp.dot(
                jnp.concatenate([left, right], axis=1), weight, preferred_element_type=F32
            ).astype(BF16)
            for k in range(SIDE):
                outs[k][quad * 16 : (quad + 1) * 16, :] = got[k * 16 : (k + 1) * 16]


def grow(shrunk, own, other, count):
    return pl.pallas_call(
        grow_kernel,
        name="grow",
        out_shape=[jax.ShapeDtypeStruct((count, own.shape[1]), BF16)] * SIDE,
        in_specs=whole(3),
        out_specs=whole(SIDE),
        compiler_params=pltpu.CompilerParams(vmem_limit_bytes=VMEM_BYTES),
        cost_estimate=pl.CostEstimate(flops=2**28, bytes_accessed=2**22, transcendentals=0),
    )(shrunk, own, other)


def collect_kernel(slot_ref, r0, r1, r2, r3, o_ref):
    count = r0.shape[0]
    blocks, rows, cols = o_ref.shape
    total = jnp.zeros((blocks * rows, cols), F32)
    for k, ref in enumerate((r0, r1, r2, r3)):
        slots = lax.broadcasted_iota(jnp.int32, (blocks * rows, count), 1) + k * count
        placing = (slots == slot_ref[...]).astype(F32).astype(BF16)
        total = total + jnp.dot(placing, ref[...], preferred_element_type=F32)
    for t in range(blocks):
        o_ref[t] = total[t * rows : (t + 1) * rows].astype(BF16)


def collect(slot, returned, blocks):
    rows = slot.shape[0]
    cols = returned[0].shape[1]
    return pl.pallas_call(
        collect_kernel,
        name="collect",
        out_shape=jax.ShapeDtypeStruct((blocks, rows // blocks, cols), BF16),
        in_specs=whole(5),
        out_specs=whole(1)[0],
        compiler_params=pltpu.CompilerParams(vmem_limit_bytes=VMEM_BYTES),
        cost_estimate=pl.CostEstimate(flops=2**28, bytes_accessed=2**21, transcendentals=0),
    )(slot.reshape(rows, 1), *returned)


def finish_kernel(skip_ref, s_ref, a_ref, b_ref, c_ref, delta_ref, o_ref):
    blocks, _, cols = delta_ref.shape
    for t in range(blocks):
        at = slice(t * cols, (t + 1) * cols)
        base = (
            s_ref[:, at]
            + a_ref[:, at].astype(F32)
            + b_ref[:, at].astype(F32)
            + c_ref[:, at].astype(F32)
        )
        o_ref[:, at] = (
            skip_ref[:, at].astype(F32) + base + 2.0 * delta_ref[t].astype(F32)
        ).astype(BF16)


def finish(*operands):
    return pl.pallas_call(
        finish_kernel,
        name="finish",
        out_shape=jax.ShapeDtypeStruct(operands[0].shape, BF16),
        in_specs=whole(6),
        out_specs=whole(1)[0],
        compiler_params=pltpu.CompilerParams(vmem_limit_bytes=VMEM_BYTES),
        cost_estimate=pl.CostEstimate(flops=2**20, bytes_accessed=2**21, transcendentals=0),
    )(*operands)


def wide_sum(*terms):
    return sum(term.astype(F32) for term in terms)


def body(
    queries,
    cached_key_rows,
    cached_value_rows,
    fresh_key,
    fresh_value,
    lengths,
    adapter_index,
    skip_stream,
    output_weight,
    adapter_down_weight,
    adapter_up_weight,
):
    blocks = lax.axis_size("tp")
    rep, tp = lax.axis_index("rep"), lax.axis_index("tp")
    held, depth, rank = adapter_down_weight.shape
    width = output_weight.shape[1]

    down_own = jnp.swapaxes(adapter_down_weight, 1, 2).reshape(held * rank, depth)
    up_own = adapter_up_weight.reshape(held * rank, depth)
    down_other = pass_core(down_own)
    up_other = pass_core(up_own)

    adapter = adapter_index[:, 0]
    rows = adapter.shape[0]
    same = adapter[:, None] == adapter[None, :]
    count_up = jnp.arange(rows, dtype=jnp.int32)
    ranked = jnp.sum((same & (count_up[:, None] > count_up[None, :])).astype(jnp.int32), axis=1)
    owner = adapter // held
    cap = 4
    per_z = 2 * held * cap
    slot = (
        (owner // 2 - rep // 2) % SIDE * per_z
        + ((owner % 2) ^ (rep % 2)) * (held * cap)
        + (adapter % held) * cap
        + ranked
    )
    order = lax.dynamic_slice(jnp.asarray(row_order()), (rep * blocks + tp, 0), (1, blocks))[0]

    attended = attend(
        queries, cached_key_rows, cached_value_rows, fresh_key, fresh_value, lengths, blocks
    )
    features = lax.all_to_all(attended, "tp", split_axis=0, concat_axis=0, tiled=True)
    flat = features.reshape(rows, depth)

    placed = dispatch(slot, flat, per_z)
    arrived = [placed[0]] + [pass_z(placed[k], k) for k in range(1, SIDE)]

    partial = project(order, features, output_weight)
    first = [pass_plane(partial[k], "xy", k) for k in range(1, SIDE)]

    shrunk = shrink(arrived, down_own, down_other)
    for axis in ("xx", "yy"):
        shrunk = wide_sum(shrunk, *[pass_plane(shrunk, axis, k) for k in range(1, SIDE)]).astype(
            BF16
        )
    grown = grow(shrunk, up_own, up_other, per_z)
    returned = [grown[0]] + [pass_z(grown[k], -k) for k in range(1, SIDE)]
    delta = collect(slot, returned, blocks)

    summed = wide_sum(partial[0], *first).reshape(SIDE, rows // blocks, width)
    narrow = summed.astype(BF16)
    second = [pass_plane(narrow[k], "yx", k) for k in range(1, SIDE)]
    delta = lax.all_to_all(delta, "tp", split_axis=0, concat_axis=0, tiled=True)
    return finish(skip_stream, summed[0], *second, delta)


def solution(mesh):
    return jax.shard_map(
        body,
        mesh=mesh,
        in_specs=(
            P(BOTH, None, None),
            P(BOTH, None, None, None),
            P(BOTH, None, None, None),
            P(BOTH, None, None),
            P(BOTH, None, None),
            P(BOTH),
            P("rep", None),
            P(BOTH, None),
            P("tp", None),
            P("rep", "tp", None),
            P("rep", None, "tp"),
        ),
        out_specs=P(BOTH, None),
        check_vma=False,
    )
```

```python
import math

import jax
import jax.numpy as jnp
import numpy as np
from jax import lax
from jax.experimental import pallas as pl
from jax.experimental.pallas import tpu as pltpu
from jax.sharding import PartitionSpec as P

F32 = jnp.float32
BF16 = jnp.bfloat16
BOTH = ("rep", "tp")
SIDE = 4
VMEM_BYTES = 24 * 1024 * 1024
FULL_VMEM = 60 * 1024 * 1024


def place(z, c, y, x):
    return ((z * 2 + c) * SIDE + y) * SIDE + x


PLACES = [
    (z, c, y, x) for z in range(SIDE) for c in range(2) for y in range(SIDE) for x in range(SIDE)
]


def pass_plane(value, axis_of_core, offset):
    pairs = []
    for z, c, y, x in PLACES:
        if axis_of_core[c] == "x":
            to = place(z, c, y, (x + offset) % SIDE)
        else:
            to = place(z, c, (y + offset) % SIDE, x)
        pairs.append((place(z, c, y, x), to))
    return lax.ppermute(value, BOTH, pairs)


def pass_z(value, offset):
    pairs = [(place(z, c, y, x), place((z + offset) % SIDE, c, y, x)) for z, c, y, x in PLACES]
    return lax.ppermute(value, BOTH, pairs)


def pass_core(value):
    return lax.ppermute(
        value, BOTH, [(place(z, c, y, x), place(z, 1 - c, y, x)) for z, c, y, x in PLACES]
    )


def row_order():
    table = np.zeros((len(PLACES), SIDE * SIDE), np.int32)
    for z, c, y, x in PLACES:
        for first in range(SIDE):
            for second in range(SIDE):
                dx, dy = (first, second) if c == 0 else (second, first)
                table[place(z, c, y, x), first * SIDE + second] = (
                    (y + dy) % SIDE * SIDE + (x + dx) % SIDE
                )
    return table


AT_ONCE = 4


def attend_kernel(
    lengths_ref, q_ref, k_hbm, v_hbm, fk_ref, fv_ref, o_ref, k_ref, v_ref, mixed_ref, k_sem, v_sem
):
    rows, heads, width = q_ref.shape
    groups, span = k_ref.shape[1], k_ref.shape[2]
    fold = heads // groups
    steps = rows // AT_ONCE
    factor = 1.0 / math.sqrt(width)
    nt = (((1,), (1,)), ((), ()))

    def copy(step, far, near, sem):
        at = pl.ds(step * AT_ONCE, AT_ONCE)
        return pltpu.make_async_copy(far.at[at], near.at[at], sem.at[step])

    for step in range(steps):
        copy(step, k_hbm, k_ref, k_sem).start()
        copy(step, v_hbm, v_ref, v_sem).start()

    def one_step(step, carry):
        copy(step, k_hbm, k_ref, k_sem).wait()
        all_scores = []
        for item in range(AT_ONCE):
            row = step * AT_ONCE + item
            q = q_ref[row]
            parts = []
            for g in range(groups):
                two = q[(g // 2) * 2 * fold : (g // 2 + 1) * 2 * fold]
                got = lax.dot_general(two, k_ref[row, g], nt, preferred_element_type=F32)
                parts.append(got[(g % 2) * fold : (g % 2 + 1) * fold])
            all_scores.append(jnp.concatenate(parts, axis=0) * factor)
        copy(step, v_hbm, v_ref, v_sem).wait()
        for item in range(AT_ONCE):
            row = step * AT_ONCE + item
            scores = all_scores[item]
            fresh_k = jnp.broadcast_to(
                fk_ref[row].astype(F32)[:, None, :], (groups, fold, width)
            ).reshape(heads, width)
            own = jnp.sum(q_ref[row].astype(F32) * fresh_k, axis=-1, keepdims=True) * factor
            position = lax.broadcasted_iota(jnp.int32, (heads, span), 1)
            masked = jnp.where(position < lengths_ref[row], scores, -jnp.inf)
            top = jnp.maximum(jnp.max(masked, axis=-1, keepdims=True), own)
            expo = jnp.exp(masked - top)
            expo_own = jnp.exp(own - top)
            inverse = 1.0 / (jnp.sum(expo, axis=-1, keepdims=True) + expo_own)
            probs = (expo * inverse).astype(BF16)
            probs_own = (expo_own * inverse).astype(BF16).astype(F32)
            parts = []
            for g in range(groups):
                two = probs[(g // 2) * 2 * fold : (g // 2 + 1) * 2 * fold]
                got = jnp.dot(two, v_ref[row, g], preferred_element_type=F32)
                parts.append(got[(g % 2) * fold : (g % 2 + 1) * fold])
            fresh_v = jnp.broadcast_to(
                fv_ref[row].astype(F32)[:, None, :], (groups, fold, width)
            ).reshape(heads, width)
            mixed = jnp.concatenate(parts, axis=0) + probs_own * fresh_v
            mixed_ref[pl.ds(pl.multiple_of(row * heads, heads), heads), :] = mixed
        return carry

    lax.fori_loop(0, steps, one_step, 0)
    per_block = o_ref.shape[2] // width
    for h in range(heads):
        tile = jnp.concatenate(
            [
                mixed_ref[pl.ds(half * 8 * heads + h, 8, stride=heads), :]
                for half in range(rows // 8)
            ],
            axis=0,
        )
        lane = (h % per_block) * width
        o_ref[h // per_block, :, lane : lane + width] = tile.astype(BF16)


def attend(queries, keys, values, fresh_key, fresh_value, lengths, blocks):
    rows, heads, width = queries.shape
    vmem = pl.BlockSpec(memory_space=pltpu.VMEM)
    far = pl.BlockSpec(memory_space=pl.ANY)
    return pl.pallas_call(
        attend_kernel,
        name="attend",
        out_shape=jax.ShapeDtypeStruct((blocks, rows, heads * width // blocks), BF16),
        in_specs=[pl.BlockSpec(memory_space=pltpu.SMEM), vmem, far, far, vmem, vmem],
        out_specs=vmem,
        scratch_shapes=[
            pltpu.VMEM(keys.shape, BF16),
            pltpu.VMEM(values.shape, BF16),
            pltpu.VMEM((rows * heads, width), F32),
            pltpu.SemaphoreType.DMA((rows // AT_ONCE,)),
            pltpu.SemaphoreType.DMA((rows // AT_ONCE,)),
        ],
        compiler_params=pltpu.CompilerParams(vmem_limit_bytes=FULL_VMEM),
        cost_estimate=pl.CostEstimate(
            flops=4 * keys.size * heads // keys.shape[1],
            bytes_accessed=4 * keys.size,
            transcendentals=0,
        ),
    )(lengths, queries, keys, values, fresh_key, fresh_value)


def whole(count):
    return [pl.BlockSpec(memory_space=pltpu.VMEM)] * count


TILES = 8


def project_kernel(order_ref, f_ref, w_ref, own, ahead, back, ahead_last, back_last, *scratch):
    rows_ref, out_ref, o_sem = scratch
    block = f_ref.shape[1]
    tile = w_ref.shape[1] // TILES
    chunk = rows_ref.shape[0] // SIDE
    half = TILES // 2

    def departure(k, part):
        low = k < half
        to = (
            own,
            ahead_last if low else ahead,
            ahead if low else back,
            back if low else back_last,
        )[part]
        column = (k if to.shape[1] == tile * TILES else k % half) * tile
        return pltpu.make_async_copy(
            out_ref.at[k, pl.ds(part * chunk, chunk)],
            to.at[:, pl.ds(column, tile)],
            o_sem.at[k, part],
        )

    for k in range(SIDE * SIDE):
        rows_ref[k * block : (k + 1) * block, :] = f_ref[order_ref[k]]
    for k in range(TILES):
        out_ref[k] = jnp.dot(
            rows_ref[...], w_ref[:, k * tile : (k + 1) * tile], preferred_element_type=F32
        ).astype(BF16)
        for part in range(SIDE):
            departure(k, part).start()
    for k in range(TILES):
        for part in range(SIDE):
            departure(k, part).wait()


def project(order, features, weight):
    blocks, rows, depth = features.shape
    cols = weight.shape[1]
    tile = cols // TILES
    chunk = blocks * rows // SIDE
    far = pl.BlockSpec(memory_space=pl.ANY)
    full = jax.ShapeDtypeStruct((chunk, cols), BF16)
    part = jax.ShapeDtypeStruct((chunk, cols // 2), BF16)
    return pl.pallas_call(
        project_kernel,
        name="project",
        out_shape=[full, full, full, part, part],
        in_specs=[
            pl.BlockSpec(memory_space=pltpu.SMEM),
            pl.BlockSpec(memory_space=pltpu.VMEM),
            pl.BlockSpec(memory_space=pltpu.VMEM),
        ],
        out_specs=[far] * 5,
        scratch_shapes=[
            pltpu.VMEM((blocks * rows, depth), BF16),
            pltpu.VMEM((TILES, blocks * rows, tile), BF16),
            pltpu.SemaphoreType.DMA((TILES, SIDE)),
        ],
        compiler_params=pltpu.CompilerParams(vmem_limit_bytes=VMEM_BYTES),
        cost_estimate=pl.CostEstimate(
            flops=2 * blocks * rows * depth * cols,
            bytes_accessed=2 * depth * cols + 2 * blocks * rows * cols,
            transcendentals=0,
        ),
    )(order, features, weight)


def meet_kernel(ahead_last, back_last, came_ahead, came_back, ahead_ref, back_ref):
    half = ahead_ref.shape[1]
    ahead_ref[...] = (ahead_last[...].astype(F32) + came_ahead[:, :half].astype(F32)).astype(BF16)
    back_ref[...] = (back_last[...].astype(F32) + came_back[:, half:].astype(F32)).astype(BF16)


def meet(*operands):
    return pl.pallas_call(
        meet_kernel,
        name="meet",
        out_shape=[jax.ShapeDtypeStruct(operands[0].shape, BF16)] * 2,
        in_specs=whole(4),
        out_specs=whole(2),
        compiler_params=pltpu.CompilerParams(vmem_limit_bytes=VMEM_BYTES),
        cost_estimate=pl.CostEstimate(flops=2**20, bytes_accessed=2**22, transcendentals=0),
    )(*operands)


def join_kernel(own, came_ahead, came_back, ahead_last, back_last, *outs):
    rows = outs[0].shape[0]
    half = ahead_last.shape[1]
    for k in range(SIDE):
        at = slice(k * rows, (k + 1) * rows)
        for right in range(2):
            cols = slice(right * half, (right + 1) * half)
            total = own[at, cols].astype(F32)
            if right:
                total = total + came_ahead[at, cols].astype(F32) + back_last[at].astype(F32)
            else:
                total = total + ahead_last[at].astype(F32) + came_back[at, cols].astype(F32)
            outs[k][:, cols] = total.astype(BF16)


def join(*operands):
    rows, cols = operands[0].shape
    return pl.pallas_call(
        join_kernel,
        name="join",
        out_shape=[jax.ShapeDtypeStruct((rows // SIDE, cols), BF16)] * SIDE,
        in_specs=whole(5),
        out_specs=whole(SIDE),
        compiler_params=pltpu.CompilerParams(vmem_limit_bytes=VMEM_BYTES),
        cost_estimate=pl.CostEstimate(flops=2**20, bytes_accessed=2**22, transcendentals=0),
    )(*operands)


def dispatch_kernel(slot_ref, f_ref, _down, _up, *outs):
    count = outs[0].shape[0]
    rows = f_ref.shape[0]
    features = f_ref[...]
    for k in range(SIDE):
        slots = lax.broadcasted_iota(jnp.int32, (count, rows), 0) + k * count
        placing = (slots == slot_ref[...]).astype(F32).astype(BF16)
        outs[k][...] = jnp.dot(placing, features, preferred_element_type=F32).astype(BF16)


def dispatch(slot, features, count, down, up):
    rows, depth = features.shape
    return pl.pallas_call(
        dispatch_kernel,
        name="dispatch",
        out_shape=[jax.ShapeDtypeStruct((count, depth), BF16)] * SIDE,
        in_specs=whole(2) + [pl.BlockSpec(memory_space=pl.ANY)] * 2,
        out_specs=whole(SIDE),
        compiler_params=pltpu.CompilerParams(vmem_limit_bytes=VMEM_BYTES),
        cost_estimate=pl.CostEstimate(
            flops=2 * SIDE * count * rows * depth,
            bytes_accessed=2 * (rows + SIDE * count) * depth,
            transcendentals=0,
        ),
    )(slot, features, down, up)


QUAD = 4


def lanes_of(rows, rank, swapped):
    row = lax.broadcasted_iota(jnp.int32, (rows, 2 * rank), 0)
    lane = lax.broadcasted_iota(jnp.int32, (rows, 2 * rank), 1)
    member = (row % 16) // QUAD
    half = (lane // rank) ^ swapped
    return (member % 2) == half, member < 2


def shrink_kernel(s0, s1, s2, s3, own_ref, other_ref, o_ref):
    rank = o_ref.shape[1] // 2
    nt = (((1,), (1,)), ((), ()))
    quads = own_ref.shape[0] // (QUAD * rank)
    for pair in range(quads):
        total = None
        for swapped, weight_ref in ((0, own_ref), (1, other_ref)):
            quad = pair + swapped * quads
            rows = jnp.concatenate([s[quad * 16 : (quad + 1) * 16, :] for s in (s0, s1, s2, s3)])
            weight = weight_ref[pair * QUAD * rank : (pair + 1) * QUAD * rank, :]
            if swapped:
                weight = jnp.concatenate(
                    [weight[(m ^ 1) * rank : ((m ^ 1) + 1) * rank] for m in range(QUAD)]
                )
            got = lax.dot_general(rows, weight, nt, preferred_element_type=F32)
            mine, first = lanes_of(rows.shape[0], rank, swapped)
            kept = jnp.where(first, got[:, : 2 * rank], got[:, 2 * rank :])
            kept = jnp.where(mine, kept, 0.0)
            total = kept if total is None else total + kept
        o_ref[pair * 64 : (pair + 1) * 64, :] = total.astype(BF16)


def shrink(slots, own, other):
    rank = 64
    return pl.pallas_call(
        shrink_kernel,
        name="shrink",
        out_shape=jax.ShapeDtypeStruct((own.shape[0] // (QUAD * rank) * 64, 2 * rank), BF16),
        in_specs=whole(6),
        out_specs=whole(1)[0],
        compiler_params=pltpu.CompilerParams(vmem_limit_bytes=VMEM_BYTES),
        cost_estimate=pl.CostEstimate(flops=2**28, bytes_accessed=2**22, transcendentals=0),
    )(*slots, own, other)


def grow_kernel(h_ref, own_ref, other_ref, *outs):
    rank = h_ref.shape[1] // 2
    quads = own_ref.shape[0] // (QUAD * rank)
    for pair in range(quads):
        held = h_ref[pair * 64 : (pair + 1) * 64, :].astype(F32)
        for swapped, weight_ref in ((0, own_ref), (1, other_ref)):
            quad = pair + swapped * quads
            weight = weight_ref[pair * QUAD * rank : (pair + 1) * QUAD * rank, :]
            if swapped:
                weight = jnp.concatenate(
                    [weight[(m ^ 1) * rank : ((m ^ 1) + 1) * rank] for m in range(QUAD)]
                )
            mine, first = lanes_of(held.shape[0], rank, swapped)
            left = jnp.where(mine & first, held, 0.0).astype(BF16)
            right = jnp.where(mine & ~first, held, 0.0).astype(BF16)
            got = jnp.dot(
                jnp.concatenate([left, right], axis=1), weight, preferred_element_type=F32
            ).astype(BF16)
            for k in range(SIDE):
                outs[k][quad * 16 : (quad + 1) * 16, :] = got[k * 16 : (k + 1) * 16]


def grow(shrunk, own, other, count):
    return pl.pallas_call(
        grow_kernel,
        name="grow",
        out_shape=[jax.ShapeDtypeStruct((count, own.shape[1]), BF16)] * SIDE,
        in_specs=whole(3),
        out_specs=whole(SIDE),
        compiler_params=pltpu.CompilerParams(vmem_limit_bytes=VMEM_BYTES),
        cost_estimate=pl.CostEstimate(flops=2**28, bytes_accessed=2**22, transcendentals=0),
    )(shrunk, own, other)


def collect_kernel(slot_ref, r0, r1, r2, r3, o_ref):
    count = r0.shape[0]
    blocks, rows, cols = o_ref.shape
    total = jnp.zeros((blocks * rows, cols), F32)
    for k, ref in enumerate((r0, r1, r2, r3)):
        slots = lax.broadcasted_iota(jnp.int32, (count, blocks * rows), 0) + k * count
        placing = (slots == slot_ref[...]).astype(F32).astype(BF16)
        total = total + lax.dot_general(
            placing, ref[...], (((0,), (0,)), ((), ())), preferred_element_type=F32
        )
    for t in range(blocks):
        o_ref[t] = total[t * rows : (t + 1) * rows].astype(BF16)


def collect(slot, returned, blocks):
    rows = slot.shape[1]
    cols = returned[0].shape[1]
    return pl.pallas_call(
        collect_kernel,
        name="collect",
        out_shape=jax.ShapeDtypeStruct((blocks, rows // blocks, cols), BF16),
        in_specs=whole(5),
        out_specs=whole(1)[0],
        compiler_params=pltpu.CompilerParams(vmem_limit_bytes=VMEM_BYTES),
        cost_estimate=pl.CostEstimate(flops=2**28, bytes_accessed=2**21, transcendentals=0),
    )(slot, *returned)


def finish_kernel(skip_ref, s_ref, a_ref, b_ref, c_ref, delta_ref, o_ref):
    blocks, _, cols = delta_ref.shape
    for t in range(blocks):
        at = slice(t * cols, (t + 1) * cols)
        base = (
            s_ref[:, at].astype(F32)
            + a_ref[:, at].astype(F32)
            + b_ref[:, at].astype(F32)
            + c_ref[:, at].astype(F32)
        )
        o_ref[:, at] = (
            skip_ref[:, at].astype(F32) + base + 2.0 * delta_ref[t].astype(F32)
        ).astype(BF16)


def finish(*operands):
    rows_of = operands[0].shape
    return pl.pallas_call(
        finish_kernel,
        name="finish",
        out_shape=jax.ShapeDtypeStruct(operands[0].shape, BF16),
        grid=(1,),
        in_specs=[
            pl.BlockSpec(rows_of, lambda i: (0, 0)),
            pl.BlockSpec(rows_of, lambda i: (0, 0)),
            pl.BlockSpec(rows_of, lambda i: (0, 0)),
            pl.BlockSpec(rows_of, lambda i: (0, 0)),
            pl.BlockSpec(rows_of, lambda i: (0, 0)),
            pl.BlockSpec(operands[5].shape, lambda i: (0, 0, 0)),
        ],
        out_specs=pl.BlockSpec(rows_of, lambda i: (0, 0)),
        compiler_params=pltpu.CompilerParams(vmem_limit_bytes=VMEM_BYTES),
        cost_estimate=pl.CostEstimate(flops=2**20, bytes_accessed=2**21, transcendentals=0),
    )(*operands)


def wide_sum(*terms):
    return sum(term.astype(F32) for term in terms)


def body(
    queries,
    cached_key_rows,
    cached_value_rows,
    fresh_key,
    fresh_value,
    lengths,
    adapter_index,
    skip_stream,
    output_weight,
    adapter_down_weight,
    adapter_up_weight,
):
    blocks = lax.axis_size("tp")
    rep, tp = lax.axis_index("rep"), lax.axis_index("tp")
    held, depth, rank = adapter_down_weight.shape
    width = output_weight.shape[1]

    down_own = jnp.swapaxes(adapter_down_weight, 1, 2).reshape(held * rank, depth)
    up_own = adapter_up_weight.reshape(held * rank, depth)
    down_other = pass_core(down_own)
    up_other = pass_core(up_own)

    adapter = adapter_index[:, 0]
    rows = adapter.shape[0]
    same = adapter[:, None] == adapter[None, :]
    count_up = jnp.arange(rows, dtype=jnp.int32)
    ranked = jnp.sum((same & (count_up[:, None] > count_up[None, :])).astype(jnp.int32), axis=1)
    owner = adapter // held
    cap = 4
    per_z = 2 * held * cap
    slot = (
        (owner // 2 - rep // 2) % SIDE * per_z
        + ((owner % 2) ^ (rep % 2)) * (held * cap)
        + (adapter % held) * cap
        + ranked
    ).reshape(1, rows)
    order = lax.dynamic_slice(jnp.asarray(row_order()), (rep * blocks + tp, 0), (1, blocks))[0]

    attended = attend(
        queries, cached_key_rows, cached_value_rows, fresh_key, fresh_value, lengths, blocks
    )
    features = lax.all_to_all(attended, "tp", split_axis=0, concat_axis=0, tiled=True)
    flat = features.reshape(rows, depth)

    placed = dispatch(slot, flat, per_z, down_other, up_other)
    arrived = [placed[0]] + [pass_z(placed[k], k) for k in range(1, SIDE)]

    own, ahead, back, ahead_last, back_last = project(order, features, output_weight)
    ahead, *arrived = lax.optimization_barrier((ahead, *arrived))
    came_ahead, came_back = pass_plane(ahead, "xy", 1), pass_plane(back, "xy", -1)

    shrunk = shrink(arrived, down_own, down_other)
    near = [pass_plane(shrunk, "yx", k) for k in range(1, SIDE)]
    shrunk = wide_sum(shrunk, *near).astype(BF16)
    near = [pass_plane(shrunk, "xy", k) for k in range(1, SIDE)]
    *near, ahead_last, back_last = lax.optimization_barrier((*near, ahead_last, back_last))
    shrunk = wide_sum(shrunk, *near).astype(BF16)
    ahead_last, back_last = meet(ahead_last, back_last, came_ahead, came_back)
    ahead_last, back_last = pass_plane(ahead_last, "xy", 1), pass_plane(back_last, "xy", -1)
    grown = grow(shrunk, up_own, up_other, per_z)
    returned = [grown[0]] + [pass_z(grown[k], -k) for k in range(1, SIDE)]
    delta = collect(slot, returned, blocks)

    summed = join(own, came_ahead, came_back, ahead_last, back_last)
    second = [pass_plane(summed[k], "yx", k) for k in range(1, SIDE)]
    delta = lax.all_to_all(delta, "tp", split_axis=0, concat_axis=0, tiled=True)
    return finish(skip_stream, summed[0], *second, delta)


def solution(mesh):
    return jax.shard_map(
        body,
        mesh=mesh,
        in_specs=(
            P(BOTH, None, None),
            P(BOTH, None, None, None),
            P(BOTH, None, None, None),
            P(BOTH, None, None),
            P(BOTH, None, None),
            P(BOTH),
            P("rep", None),
            P(BOTH, None),
            P("tp", None),
            P("rep", "tp", None),
            P("rep", None, "tp"),
        ),
        out_specs=P(BOTH, None),
        check_vma=False,
    )
```

```python
import math

import jax
import jax.numpy as jnp
import numpy as np
from jax import lax
from jax.experimental import pallas as pl
from jax.experimental.pallas import tpu as pltpu
from jax.sharding import PartitionSpec as P

F32 = jnp.float32
BF16 = jnp.bfloat16
BOTH = ("rep", "tp")
SIDE = 4
VMEM_BYTES = 24 * 1024 * 1024
FULL_VMEM = 60 * 1024 * 1024


def place(z, c, y, x):
    return ((z * 2 + c) * SIDE + y) * SIDE + x


PLACES = [
    (z, c, y, x) for z in range(SIDE) for c in range(2) for y in range(SIDE) for x in range(SIDE)
]


def pass_plane(value, axis_of_core, offset):
    pairs = []
    for z, c, y, x in PLACES:
        if axis_of_core[c] == "x":
            to = place(z, c, y, (x + offset) % SIDE)
        else:
            to = place(z, c, (y + offset) % SIDE, x)
        pairs.append((place(z, c, y, x), to))
    return lax.ppermute(value, BOTH, pairs)


def pass_z(value, offset):
    pairs = [(place(z, c, y, x), place((z + offset) % SIDE, c, y, x)) for z, c, y, x in PLACES]
    return lax.ppermute(value, BOTH, pairs)


def pass_core(value):
    return lax.ppermute(
        value, BOTH, [(place(z, c, y, x), place(z, 1 - c, y, x)) for z, c, y, x in PLACES]
    )


def row_order():
    table = np.zeros((len(PLACES), SIDE * SIDE), np.int32)
    for z, c, y, x in PLACES:
        for first in range(SIDE):
            for second in range(SIDE):
                dx, dy = (first, second) if c == 0 else (second, first)
                table[place(z, c, y, x), first * SIDE + second] = (
                    (y + dy) % SIDE * SIDE + (x + dx) % SIDE
                )
    return table


AT_ONCE = 4


def attend_kernel(
    lengths_ref, q_ref, k_hbm, v_hbm, fk_ref, fv_ref, o_ref, k_ref, v_ref, mixed_ref, k_sem, v_sem
):
    rows, heads, width = q_ref.shape
    groups, span = k_ref.shape[1], k_ref.shape[2]
    fold = heads // groups
    steps = rows // AT_ONCE
    factor = 1.0 / math.sqrt(width)
    nt = (((1,), (1,)), ((), ()))

    def copy(step, far, near, sem):
        at = pl.ds(step * AT_ONCE, AT_ONCE)
        return pltpu.make_async_copy(far.at[at], near.at[at], sem.at[step])

    for step in range(steps):
        copy(step, k_hbm, k_ref, k_sem).start()
        copy(step, v_hbm, v_ref, v_sem).start()

    def one_step(step, carry):
        copy(step, k_hbm, k_ref, k_sem).wait()
        all_scores = []
        for item in range(AT_ONCE):
            row = step * AT_ONCE + item
            q = q_ref[row]
            parts = []
            for g in range(groups):
                two = q[(g // 2) * 2 * fold : (g // 2 + 1) * 2 * fold]
                got = lax.dot_general(two, k_ref[row, g], nt, preferred_element_type=F32)
                parts.append(got[(g % 2) * fold : (g % 2 + 1) * fold])
            all_scores.append(jnp.concatenate(parts, axis=0) * factor)
        copy(step, v_hbm, v_ref, v_sem).wait()
        for item in range(AT_ONCE):
            row = step * AT_ONCE + item
            scores = all_scores[item]
            fresh_k = jnp.broadcast_to(
                fk_ref[row].astype(F32)[:, None, :], (groups, fold, width)
            ).reshape(heads, width)
            own = jnp.sum(q_ref[row].astype(F32) * fresh_k, axis=-1, keepdims=True) * factor
            position = lax.broadcasted_iota(jnp.int32, (heads, span), 1)
            masked = jnp.where(position < lengths_ref[row], scores, -jnp.inf)
            top = jnp.maximum(jnp.max(masked, axis=-1, keepdims=True), own)
            expo = jnp.exp(masked - top)
            expo_own = jnp.exp(own - top)
            inverse = 1.0 / (jnp.sum(expo, axis=-1, keepdims=True) + expo_own)
            probs = (expo * inverse).astype(BF16)
            probs_own = (expo_own * inverse).astype(BF16).astype(F32)
            parts = []
            for g in range(groups):
                two = probs[(g // 2) * 2 * fold : (g // 2 + 1) * 2 * fold]
                got = jnp.dot(two, v_ref[row, g], preferred_element_type=F32)
                parts.append(got[(g % 2) * fold : (g % 2 + 1) * fold])
            fresh_v = jnp.broadcast_to(
                fv_ref[row].astype(F32)[:, None, :], (groups, fold, width)
            ).reshape(heads, width)
            mixed = jnp.concatenate(parts, axis=0) + probs_own * fresh_v
            mixed_ref[pl.ds(pl.multiple_of(row * heads, heads), heads), :] = mixed
        return carry

    lax.fori_loop(0, steps, one_step, 0)
    per_block = o_ref.shape[2] // width
    for h in range(heads):
        tile = jnp.concatenate(
            [
                mixed_ref[pl.ds(half * 8 * heads + h, 8, stride=heads), :]
                for half in range(rows // 8)
            ],
            axis=0,
        )
        lane = (h % per_block) * width
        o_ref[h // per_block, :, lane : lane + width] = tile.astype(BF16)


def attend(queries, keys, values, fresh_key, fresh_value, lengths, blocks):
    rows, heads, width = queries.shape
    vmem = pl.BlockSpec(memory_space=pltpu.VMEM)
    far = pl.BlockSpec(memory_space=pl.ANY)
    return pl.pallas_call(
        attend_kernel,
        name="attend",
        out_shape=jax.ShapeDtypeStruct((blocks, rows, heads * width // blocks), BF16),
        in_specs=[pl.BlockSpec(memory_space=pltpu.SMEM), vmem, far, far, vmem, vmem],
        out_specs=vmem,
        scratch_shapes=[
            pltpu.VMEM(keys.shape, BF16),
            pltpu.VMEM(values.shape, BF16),
            pltpu.VMEM((rows * heads, width), F32),
            pltpu.SemaphoreType.DMA((rows // AT_ONCE,)),
            pltpu.SemaphoreType.DMA((rows // AT_ONCE,)),
        ],
        compiler_params=pltpu.CompilerParams(vmem_limit_bytes=FULL_VMEM),
        cost_estimate=pl.CostEstimate(
            flops=4 * keys.size * heads // keys.shape[1],
            bytes_accessed=4 * keys.size,
            transcendentals=0,
        ),
    )(lengths, queries, keys, values, fresh_key, fresh_value)


def whole(count):
    return [pl.BlockSpec(memory_space=pltpu.VMEM)] * count


TILES = 8


def project_kernel(order_ref, f_ref, w_ref, own, ahead, back, ahead_last, back_last, *scratch):
    rows_ref, out_ref, o_sem = scratch
    block = f_ref.shape[1]
    tile = w_ref.shape[1] // TILES
    chunk = rows_ref.shape[0] // SIDE
    half = TILES // 2

    def departure(k, part):
        low = k < half
        to = (
            own,
            ahead_last if low else ahead,
            ahead if low else back,
            back if low else back_last,
        )[part]
        column = (k if to.shape[1] == tile * TILES else k % half) * tile
        return pltpu.make_async_copy(
            out_ref.at[k, pl.ds(part * chunk, chunk)],
            to.at[:, pl.ds(column, tile)],
            o_sem.at[k, part],
        )

    for k in range(SIDE * SIDE):
        rows_ref[k * block : (k + 1) * block, :] = f_ref[order_ref[k]]
    for k in range(TILES):
        out_ref[k] = jnp.dot(
            rows_ref[...], w_ref[:, k * tile : (k + 1) * tile], preferred_element_type=F32
        ).astype(BF16)
        for part in range(SIDE):
            departure(k, part).start()
    for k in range(TILES):
        for part in range(SIDE):
            departure(k, part).wait()


def project(order, features, weight):
    blocks, rows, depth = features.shape
    cols = weight.shape[1]
    tile = cols // TILES
    chunk = blocks * rows // SIDE
    far = pl.BlockSpec(memory_space=pl.ANY)
    full = jax.ShapeDtypeStruct((chunk, cols), BF16)
    part = jax.ShapeDtypeStruct((chunk, cols // 2), BF16)
    return pl.pallas_call(
        project_kernel,
        name="project",
        out_shape=[full, full, full, part, part],
        in_specs=[
            pl.BlockSpec(memory_space=pltpu.SMEM),
            pl.BlockSpec(memory_space=pltpu.VMEM),
            pl.BlockSpec(memory_space=pltpu.VMEM),
        ],
        out_specs=[far] * 5,
        scratch_shapes=[
            pltpu.VMEM((blocks * rows, depth), BF16),
            pltpu.VMEM((TILES, blocks * rows, tile), BF16),
            pltpu.SemaphoreType.DMA((TILES, SIDE)),
        ],
        compiler_params=pltpu.CompilerParams(vmem_limit_bytes=VMEM_BYTES),
        cost_estimate=pl.CostEstimate(
            flops=2 * blocks * rows * depth * cols,
            bytes_accessed=2 * depth * cols + 2 * blocks * rows * cols,
            transcendentals=0,
        ),
    )(order, features, weight)


def meet_kernel(ahead_last, back_last, came_ahead, came_back, ahead_ref, back_ref):
    half = ahead_ref.shape[1]
    ahead_ref[...] = (ahead_last[...].astype(F32) + came_ahead[:, :half].astype(F32)).astype(BF16)
    back_ref[...] = (back_last[...].astype(F32) + came_back[:, half:].astype(F32)).astype(BF16)


def meet(*operands):
    return pl.pallas_call(
        meet_kernel,
        name="meet",
        out_shape=[jax.ShapeDtypeStruct(operands[0].shape, BF16)] * 2,
        in_specs=whole(4),
        out_specs=whole(2),
        compiler_params=pltpu.CompilerParams(vmem_limit_bytes=VMEM_BYTES),
        cost_estimate=pl.CostEstimate(flops=2**20, bytes_accessed=2**22, transcendentals=0),
    )(*operands)


def join_kernel(own, came_ahead, came_back, ahead_last, back_last, *outs):
    rows = outs[0].shape[0]
    half = ahead_last.shape[1]
    for k in range(SIDE):
        at = slice(k * rows, (k + 1) * rows)
        for right in range(2):
            cols = slice(right * half, (right + 1) * half)
            total = own[at, cols].astype(F32)
            if right:
                total = total + came_ahead[at, cols].astype(F32) + back_last[at].astype(F32)
            else:
                total = total + ahead_last[at].astype(F32) + came_back[at, cols].astype(F32)
            outs[k][:, cols] = total.astype(BF16)


def join(*operands):
    rows, cols = operands[0].shape
    return pl.pallas_call(
        join_kernel,
        name="join",
        out_shape=[jax.ShapeDtypeStruct((rows // SIDE, cols), BF16)] * SIDE,
        in_specs=whole(5),
        out_specs=whole(SIDE),
        compiler_params=pltpu.CompilerParams(vmem_limit_bytes=VMEM_BYTES),
        cost_estimate=pl.CostEstimate(flops=2**20, bytes_accessed=2**22, transcendentals=0),
    )(*operands)


def dispatch_kernel(slot_ref, f_ref, _down, _up, *outs):
    count = outs[0].shape[0]
    rows = f_ref.shape[0]
    features = f_ref[...]
    for k in range(SIDE):
        slots = lax.broadcasted_iota(jnp.int32, (count, rows), 0) + k * count
        placing = (slots == slot_ref[...]).astype(F32).astype(BF16)
        outs[k][...] = jnp.dot(placing, features, preferred_element_type=F32).astype(BF16)


def dispatch(slot, features, count, down, up):
    rows, depth = features.shape
    return pl.pallas_call(
        dispatch_kernel,
        name="dispatch",
        out_shape=[jax.ShapeDtypeStruct((count, depth), BF16)] * SIDE,
        in_specs=whole(2) + [pl.BlockSpec(memory_space=pl.ANY)] * 2,
        out_specs=whole(SIDE),
        compiler_params=pltpu.CompilerParams(vmem_limit_bytes=VMEM_BYTES),
        cost_estimate=pl.CostEstimate(
            flops=2 * SIDE * count * rows * depth,
            bytes_accessed=2 * (rows + SIDE * count) * depth,
            transcendentals=0,
        ),
    )(slot, features, down, up)


QUAD = 4


def lanes_of(rows, rank, swapped):
    row = lax.broadcasted_iota(jnp.int32, (rows, 2 * rank), 0)
    lane = lax.broadcasted_iota(jnp.int32, (rows, 2 * rank), 1)
    member = (row % 16) // QUAD
    half = (lane // rank) ^ swapped
    return (member % 2) == half, member < 2


def shrink_kernel(s0, s1, s2, s3, own_ref, other_ref, o_ref):
    rank = o_ref.shape[1] // 2
    nt = (((1,), (1,)), ((), ()))
    quads = own_ref.shape[0] // (QUAD * rank)
    for pair in range(quads):
        total = None
        for swapped, weight_ref in ((0, own_ref), (1, other_ref)):
            quad = pair + swapped * quads
            rows = jnp.concatenate([s[quad * 16 : (quad + 1) * 16, :] for s in (s0, s1, s2, s3)])
            weight = weight_ref[pair * QUAD * rank : (pair + 1) * QUAD * rank, :]
            if swapped:
                weight = jnp.concatenate(
                    [weight[(m ^ 1) * rank : ((m ^ 1) + 1) * rank] for m in range(QUAD)]
                )
            got = lax.dot_general(rows, weight, nt, preferred_element_type=F32)
            mine, first = lanes_of(rows.shape[0], rank, swapped)
            kept = jnp.where(first, got[:, : 2 * rank], got[:, 2 * rank :])
            kept = jnp.where(mine, kept, 0.0)
            total = kept if total is None else total + kept
        o_ref[pair * 64 : (pair + 1) * 64, :] = total.astype(BF16)


def shrink(slots, own, other):
    rank = 64
    return pl.pallas_call(
        shrink_kernel,
        name="shrink",
        out_shape=jax.ShapeDtypeStruct((own.shape[0] // (QUAD * rank) * 64, 2 * rank), BF16),
        in_specs=whole(6),
        out_specs=whole(1)[0],
        compiler_params=pltpu.CompilerParams(vmem_limit_bytes=VMEM_BYTES),
        cost_estimate=pl.CostEstimate(flops=2**28, bytes_accessed=2**22, transcendentals=0),
    )(*slots, own, other)


def grow_kernel(h_ref, own_ref, other_ref, *outs):
    rank = h_ref.shape[1] // 2
    quads = own_ref.shape[0] // (QUAD * rank)
    for pair in range(quads):
        held = h_ref[pair * 64 : (pair + 1) * 64, :].astype(F32)
        for swapped, weight_ref in ((0, own_ref), (1, other_ref)):
            quad = pair + swapped * quads
            weight = weight_ref[pair * QUAD * rank : (pair + 1) * QUAD * rank, :]
            if swapped:
                weight = jnp.concatenate(
                    [weight[(m ^ 1) * rank : ((m ^ 1) + 1) * rank] for m in range(QUAD)]
                )
            mine, first = lanes_of(held.shape[0], rank, swapped)
            left = jnp.where(mine & first, held, 0.0).astype(BF16)
            right = jnp.where(mine & ~first, held, 0.0).astype(BF16)
            got = jnp.dot(
                jnp.concatenate([left, right], axis=1), weight, preferred_element_type=F32
            ).astype(BF16)
            for k in range(SIDE):
                outs[k][quad * 16 : (quad + 1) * 16, :] = got[k * 16 : (k + 1) * 16]


def grow(shrunk, own, other, count):
    return pl.pallas_call(
        grow_kernel,
        name="grow",
        out_shape=[jax.ShapeDtypeStruct((count, own.shape[1]), BF16)] * SIDE,
        in_specs=whole(3),
        out_specs=whole(SIDE),
        compiler_params=pltpu.CompilerParams(vmem_limit_bytes=VMEM_BYTES),
        cost_estimate=pl.CostEstimate(flops=2**28, bytes_accessed=2**22, transcendentals=0),
    )(shrunk, own, other)


def collect_kernel(slot_ref, r0, r1, r2, r3, o_ref):
    count = r0.shape[0]
    blocks, rows, cols = o_ref.shape
    total = jnp.zeros((blocks * rows, cols), F32)
    for k, ref in enumerate((r0, r1, r2, r3)):
        slots = lax.broadcasted_iota(jnp.int32, (count, blocks * rows), 0) + k * count
        placing = (slots == slot_ref[...]).astype(F32).astype(BF16)
        total = total + lax.dot_general(
            placing, ref[...], (((0,), (0,)), ((), ())), preferred_element_type=F32
        )
    for t in range(blocks):
        o_ref[t] = total[t * rows : (t + 1) * rows].astype(BF16)


def collect(slot, returned, blocks):
    rows = slot.shape[1]
    cols = returned[0].shape[1]
    return pl.pallas_call(
        collect_kernel,
        name="collect",
        out_shape=jax.ShapeDtypeStruct((blocks, rows // blocks, cols), BF16),
        in_specs=whole(5),
        out_specs=whole(1)[0],
        compiler_params=pltpu.CompilerParams(vmem_limit_bytes=VMEM_BYTES),
        cost_estimate=pl.CostEstimate(flops=2**28, bytes_accessed=2**21, transcendentals=0),
    )(slot, *returned)


def finish_kernel(skip_ref, s_ref, a_ref, b_ref, c_ref, delta_ref, o_ref):
    blocks, _, cols = delta_ref.shape
    for t in range(blocks):
        at = slice(t * cols, (t + 1) * cols)
        base = (
            s_ref[:, at].astype(F32)
            + a_ref[:, at].astype(F32)
            + b_ref[:, at].astype(F32)
            + c_ref[:, at].astype(F32)
        )
        o_ref[:, at] = (
            skip_ref[:, at].astype(F32) + base + 2.0 * delta_ref[t].astype(F32)
        ).astype(BF16)


def finish(*operands):
    rows_of = operands[0].shape
    return pl.pallas_call(
        finish_kernel,
        name="finish",
        out_shape=jax.ShapeDtypeStruct(operands[0].shape, BF16),
        grid=(1,),
        in_specs=[
            pl.BlockSpec(rows_of, lambda i: (0, 0)),
            pl.BlockSpec(rows_of, lambda i: (0, 0)),
            pl.BlockSpec(rows_of, lambda i: (0, 0)),
            pl.BlockSpec(rows_of, lambda i: (0, 0)),
            pl.BlockSpec(rows_of, lambda i: (0, 0)),
            pl.BlockSpec(operands[5].shape, lambda i: (0, 0, 0)),
        ],
        out_specs=pl.BlockSpec(rows_of, lambda i: (0, 0)),
        compiler_params=pltpu.CompilerParams(vmem_limit_bytes=VMEM_BYTES),
        cost_estimate=pl.CostEstimate(flops=2**20, bytes_accessed=2**21, transcendentals=0),
    )(*operands)


def wide_sum(*terms):
    return sum(term.astype(F32) for term in terms)


def body(
    queries,
    cached_key_rows,
    cached_value_rows,
    fresh_key,
    fresh_value,
    lengths,
    adapter_index,
    skip_stream,
    output_weight,
    adapter_down_weight,
    adapter_up_weight,
):
    blocks = lax.axis_size("tp")
    rep, tp = lax.axis_index("rep"), lax.axis_index("tp")
    held, depth, rank = adapter_down_weight.shape
    width = output_weight.shape[1]

    down_own = jnp.swapaxes(adapter_down_weight, 1, 2).reshape(held * rank, depth)
    up_own = adapter_up_weight.reshape(held * rank, depth)
    down_other = pass_core(down_own)
    up_other = pass_core(up_own)

    adapter = adapter_index[:, 0]
    rows = adapter.shape[0]
    same = adapter[:, None] == adapter[None, :]
    count_up = jnp.arange(rows, dtype=jnp.int32)
    ranked = jnp.sum((same & (count_up[:, None] > count_up[None, :])).astype(jnp.int32), axis=1)
    owner = adapter // held
    cap = 4
    per_z = 2 * held * cap
    slot = (
        (owner // 2 - rep // 2) % SIDE * per_z
        + ((owner % 2) ^ (rep % 2)) * (held * cap)
        + (adapter % held) * cap
        + ranked
    ).reshape(1, rows)
    order = lax.dynamic_slice(jnp.asarray(row_order()), (rep * blocks + tp, 0), (1, blocks))[0]

    attended = attend(
        queries, cached_key_rows, cached_value_rows, fresh_key, fresh_value, lengths, blocks
    )
    features = lax.all_to_all(attended, "tp", split_axis=0, concat_axis=0, tiled=True)
    flat = features.reshape(rows, depth)

    placed = dispatch(slot, flat, per_z, down_other, up_other)
    arrived = [placed[0]] + [pass_z(placed[k], k) for k in range(1, SIDE)]

    own, ahead, back, ahead_last, back_last = project(order, features, output_weight)
    ahead, *arrived = lax.optimization_barrier((ahead, *arrived))
    came_ahead, came_back = pass_plane(ahead, "xy", 1), pass_plane(back, "xy", -1)

    shrunk = shrink(arrived, down_own, down_other)
    near = [pass_plane(shrunk, "yx", k) for k in range(1, SIDE)]
    shrunk = wide_sum(shrunk, *near).astype(BF16)
    near = [pass_plane(shrunk, "xy", k) for k in range(1, SIDE)]
    *near, ahead_last, back_last = lax.optimization_barrier((*near, ahead_last, back_last))
    shrunk = wide_sum(shrunk, *near).astype(BF16)
    ahead_last, back_last = meet(ahead_last, back_last, came_ahead, came_back)
    ahead_last, back_last = pass_plane(ahead_last, "xy", 1), pass_plane(back_last, "xy", -1)
    grown = grow(shrunk, up_own, up_other, per_z)
    returned = [grown[0]] + [pass_z(grown[k], -k) for k in range(1, SIDE)]
    delta = collect(slot, returned, blocks)

    summed = join(own, came_ahead, came_back, ahead_last, back_last)
    *summed, delta = lax.optimization_barrier((*summed, delta))
    second = [pass_plane(summed[k], "yx", k) for k in range(1, SIDE)]
    delta = lax.all_to_all(delta, "tp", split_axis=0, concat_axis=0, tiled=True)
    return finish(skip_stream, summed[0], *second, delta)


def solution(mesh):
    return jax.shard_map(
        body,
        mesh=mesh,
        in_specs=(
            P(BOTH, None, None),
            P(BOTH, None, None, None),
            P(BOTH, None, None, None),
            P(BOTH, None, None),
            P(BOTH, None, None),
            P(BOTH),
            P("rep", None),
            P(BOTH, None),
            P("tp", None),
            P("rep", "tp", None),
            P("rep", None, "tp"),
        ),
        out_specs=P(BOTH, None),
        check_vma=False,
    )
```

```python
import math

import jax
import jax.numpy as jnp
import numpy as np
from jax import lax
from jax.experimental import pallas as pl
from jax.experimental.pallas import tpu as pltpu
from jax.sharding import PartitionSpec as P

F32 = jnp.float32
BF16 = jnp.bfloat16
BOTH = ("rep", "tp")
SIDE = 4
VMEM_BYTES = 24 * 1024 * 1024
FULL_VMEM = 60 * 1024 * 1024


def place(z, c, y, x):
    return ((z * 2 + c) * SIDE + y) * SIDE + x


PLACES = [
    (z, c, y, x) for z in range(SIDE) for c in range(2) for y in range(SIDE) for x in range(SIDE)
]


def pass_plane(value, axis_of_core, offset):
    pairs = []
    for z, c, y, x in PLACES:
        if axis_of_core[c] == "x":
            to = place(z, c, y, (x + offset) % SIDE)
        else:
            to = place(z, c, (y + offset) % SIDE, x)
        pairs.append((place(z, c, y, x), to))
    return lax.ppermute(value, BOTH, pairs)


def pass_z(value, offset):
    pairs = [(place(z, c, y, x), place((z + offset) % SIDE, c, y, x)) for z, c, y, x in PLACES]
    return lax.ppermute(value, BOTH, pairs)


def pass_core(value):
    return lax.ppermute(
        value, BOTH, [(place(z, c, y, x), place(z, 1 - c, y, x)) for z, c, y, x in PLACES]
    )


def row_order():
    table = np.zeros((len(PLACES), SIDE * SIDE), np.int32)
    for z, c, y, x in PLACES:
        for first in range(SIDE):
            for second in range(SIDE):
                dx, dy = (first, second) if c == 0 else (second, first)
                table[place(z, c, y, x), first * SIDE + second] = (
                    (y + dy) % SIDE * SIDE + (x + dx) % SIDE
                )
    return table


AT_ONCE = 4


def attend_kernel(
    lengths_ref, q_ref, k_hbm, v_hbm, fk_ref, fv_ref, o_ref, k_ref, v_ref, mixed_ref, k_sem, v_sem
):
    rows, heads, width = q_ref.shape
    groups, span = k_ref.shape[1], k_ref.shape[2]
    fold = heads // groups
    steps = rows // AT_ONCE
    factor = 1.0 / math.sqrt(width)
    nt = (((1,), (1,)), ((), ()))

    def copy(step, far, near, sem):
        at = pl.ds(step * AT_ONCE, AT_ONCE)
        return pltpu.make_async_copy(far.at[at], near.at[at], sem.at[step])

    for step in range(steps):
        copy(step, k_hbm, k_ref, k_sem).start()
        copy(step, v_hbm, v_ref, v_sem).start()

    def one_step(step, carry):
        copy(step, k_hbm, k_ref, k_sem).wait()
        all_scores = []
        for item in range(AT_ONCE):
            row = step * AT_ONCE + item
            q = q_ref[row]
            parts = []
            for g in range(groups):
                two = q[(g // 2) * 2 * fold : (g // 2 + 1) * 2 * fold]
                got = lax.dot_general(two, k_ref[row, g], nt, preferred_element_type=F32)
                parts.append(got[(g % 2) * fold : (g % 2 + 1) * fold])
            all_scores.append(jnp.concatenate(parts, axis=0) * factor)
        copy(step, v_hbm, v_ref, v_sem).wait()
        for item in range(AT_ONCE):
            row = step * AT_ONCE + item
            scores = all_scores[item]
            fresh_k = jnp.broadcast_to(
                fk_ref[row].astype(F32)[:, None, :], (groups, fold, width)
            ).reshape(heads, width)
            own = jnp.sum(q_ref[row].astype(F32) * fresh_k, axis=-1, keepdims=True) * factor
            position = lax.broadcasted_iota(jnp.int32, (heads, span), 1)
            masked = jnp.where(position < lengths_ref[row], scores, -jnp.inf)
            top = jnp.maximum(jnp.max(masked, axis=-1, keepdims=True), own)
            expo = jnp.exp(masked - top)
            expo_own = jnp.exp(own - top)
            inverse = 1.0 / (jnp.sum(expo, axis=-1, keepdims=True) + expo_own)
            probs = (expo * inverse).astype(BF16)
            probs_own = (expo_own * inverse).astype(BF16).astype(F32)
            parts = []
            for g in range(groups):
                two = probs[(g // 2) * 2 * fold : (g // 2 + 1) * 2 * fold]
                got = jnp.dot(two, v_ref[row, g], preferred_element_type=F32)
                parts.append(got[(g % 2) * fold : (g % 2 + 1) * fold])
            fresh_v = jnp.broadcast_to(
                fv_ref[row].astype(F32)[:, None, :], (groups, fold, width)
            ).reshape(heads, width)
            mixed = jnp.concatenate(parts, axis=0) + probs_own * fresh_v
            mixed_ref[pl.ds(pl.multiple_of(row * heads, heads), heads), :] = mixed
        return carry

    lax.fori_loop(0, steps, one_step, 0)
    per_block = o_ref.shape[2] // width
    for h in range(heads):
        tile = jnp.concatenate(
            [
                mixed_ref[pl.ds(half * 8 * heads + h, 8, stride=heads), :]
                for half in range(rows // 8)
            ],
            axis=0,
        )
        lane = (h % per_block) * width
        o_ref[h // per_block, :, lane : lane + width] = tile.astype(BF16)


def attend(queries, keys, values, fresh_key, fresh_value, lengths, blocks):
    rows, heads, width = queries.shape
    vmem = pl.BlockSpec(memory_space=pltpu.VMEM)
    far = pl.BlockSpec(memory_space=pl.ANY)
    return pl.pallas_call(
        attend_kernel,
        name="attend",
        out_shape=jax.ShapeDtypeStruct((blocks, rows, heads * width // blocks), BF16),
        in_specs=[pl.BlockSpec(memory_space=pltpu.SMEM), vmem, far, far, vmem, vmem],
        out_specs=vmem,
        scratch_shapes=[
            pltpu.VMEM(keys.shape, BF16),
            pltpu.VMEM(values.shape, BF16),
            pltpu.VMEM((rows * heads, width), F32),
            pltpu.SemaphoreType.DMA((rows // AT_ONCE,)),
            pltpu.SemaphoreType.DMA((rows // AT_ONCE,)),
        ],
        compiler_params=pltpu.CompilerParams(vmem_limit_bytes=FULL_VMEM),
        cost_estimate=pl.CostEstimate(
            flops=4 * keys.size * heads // keys.shape[1],
            bytes_accessed=4 * keys.size,
            transcendentals=0,
        ),
    )(lengths, queries, keys, values, fresh_key, fresh_value)


def whole(count):
    return [pl.BlockSpec(memory_space=pltpu.VMEM)] * count


TILES = 4


def project_kernel(order_ref, f_ref, w_hbm, own, ahead, back, ahead_last, back_last, *scratch):
    rows_ref, w_ref, out_ref, w_sem, o_sem = scratch
    block = f_ref.shape[1]
    tile = w_ref.shape[2]
    chunk = rows_ref.shape[0] // SIDE
    half = TILES // 2

    def arrival(k):
        return pltpu.make_async_copy(w_hbm.at[:, pl.ds(k * tile, tile)], w_ref.at[k], w_sem.at[k])

    def departure(k, part):
        low = k < half
        to = (
            own,
            ahead_last if low else ahead,
            ahead if low else back,
            back if low else back_last,
        )[part]
        column = (k if to.shape[1] == tile * TILES else k % half) * tile
        return pltpu.make_async_copy(
            out_ref.at[k, pl.ds(part * chunk, chunk)],
            to.at[:, pl.ds(column, tile)],
            o_sem.at[k, part],
        )

    for k in range(TILES):
        arrival(k).start()
    for k in range(SIDE * SIDE):
        rows_ref[k * block : (k + 1) * block, :] = f_ref[order_ref[k]]
    for k in range(TILES):
        arrival(k).wait()
        out_ref[k] = jnp.dot(rows_ref[...], w_ref[k], preferred_element_type=F32).astype(BF16)
        for part in range(SIDE):
            departure(k, part).start()
    for k in range(TILES):
        for part in range(SIDE):
            departure(k, part).wait()


def project(order, features, weight):
    blocks, rows, depth = features.shape
    cols = weight.shape[1]
    tile = cols // TILES
    chunk = blocks * rows // SIDE
    far = pl.BlockSpec(memory_space=pl.ANY)
    full = jax.ShapeDtypeStruct((chunk, cols), BF16)
    part = jax.ShapeDtypeStruct((chunk, cols // 2), BF16)
    return pl.pallas_call(
        project_kernel,
        name="project",
        out_shape=[full, full, full, part, part],
        in_specs=[
            pl.BlockSpec(memory_space=pltpu.SMEM),
            pl.BlockSpec(memory_space=pltpu.VMEM),
            far,
        ],
        out_specs=[far] * 5,
        scratch_shapes=[
            pltpu.VMEM((blocks * rows, depth), BF16),
            pltpu.VMEM((TILES, depth, tile), BF16),
            pltpu.VMEM((TILES, blocks * rows, tile), BF16),
            pltpu.SemaphoreType.DMA((TILES,)),
            pltpu.SemaphoreType.DMA((TILES, SIDE)),
        ],
        compiler_params=pltpu.CompilerParams(vmem_limit_bytes=56 * 1024 * 1024),
        cost_estimate=pl.CostEstimate(
            flops=2 * blocks * rows * depth * cols,
            bytes_accessed=2 * depth * cols + 2 * blocks * rows * cols,
            transcendentals=0,
        ),
    )(order, features, weight)


def meet_kernel(ahead_hbm, back_hbm, came_ahead, came_back, ahead_ref, back_ref, *scratch):
    ahead_last, back_last, sem = scratch
    half = ahead_ref.shape[1]
    copies = (
        pltpu.make_async_copy(ahead_hbm, ahead_last, sem.at[0]),
        pltpu.make_async_copy(back_hbm, back_last, sem.at[1]),
    )
    for copy in copies:
        copy.start()
    copies[0].wait()
    ahead_ref[...] = (ahead_last[...].astype(F32) + came_ahead[:, :half].astype(F32)).astype(BF16)
    copies[1].wait()
    back_ref[...] = (back_last[...].astype(F32) + came_back[:, half:].astype(F32)).astype(BF16)


def meet(*operands):
    half = operands[0]
    return pl.pallas_call(
        meet_kernel,
        name="meet",
        out_shape=[jax.ShapeDtypeStruct(half.shape, BF16)] * 2,
        in_specs=[pl.BlockSpec(memory_space=pl.ANY)] * 2 + whole(2),
        out_specs=whole(2),
        scratch_shapes=[
            pltpu.VMEM(half.shape, BF16),
            pltpu.VMEM(half.shape, BF16),
            pltpu.SemaphoreType.DMA((2,)),
        ],
        compiler_params=pltpu.CompilerParams(vmem_limit_bytes=VMEM_BYTES),
        cost_estimate=pl.CostEstimate(flops=2**20, bytes_accessed=2**22, transcendentals=0),
    )(*operands)


def join_kernel(own, came_ahead, came_back, ahead_last, back_last, *outs):
    rows = outs[0].shape[0]
    half = ahead_last.shape[1]
    for k in range(SIDE):
        at = slice(k * rows, (k + 1) * rows)
        for right in range(2):
            cols = slice(right * half, (right + 1) * half)
            total = own[at, cols].astype(F32)
            if right:
                total = total + came_ahead[at, cols].astype(F32) + back_last[at].astype(F32)
            else:
                total = total + ahead_last[at].astype(F32) + came_back[at, cols].astype(F32)
            outs[k][:, cols] = total.astype(BF16)


def join(*operands):
    rows, cols = operands[0].shape
    return pl.pallas_call(
        join_kernel,
        name="join",
        out_shape=[jax.ShapeDtypeStruct((rows // SIDE, cols), BF16)] * SIDE,
        in_specs=whole(5),
        out_specs=whole(SIDE),
        compiler_params=pltpu.CompilerParams(vmem_limit_bytes=VMEM_BYTES),
        cost_estimate=pl.CostEstimate(flops=2**20, bytes_accessed=2**22, transcendentals=0),
    )(*operands)


def dispatch_kernel(slot_ref, f_ref, _down, _up, *outs):
    count = outs[0].shape[0]
    rows = f_ref.shape[0]
    features = f_ref[...]
    for k in range(SIDE):
        slots = lax.broadcasted_iota(jnp.int32, (count, rows), 0) + k * count
        placing = (slots == slot_ref[...]).astype(F32).astype(BF16)
        outs[k][...] = jnp.dot(placing, features, preferred_element_type=F32).astype(BF16)


def dispatch(slot, features, count, down, up):
    rows, depth = features.shape
    return pl.pallas_call(
        dispatch_kernel,
        name="dispatch",
        out_shape=[jax.ShapeDtypeStruct((count, depth), BF16)] * SIDE,
        in_specs=whole(2) + [pl.BlockSpec(memory_space=pl.ANY)] * 2,
        out_specs=whole(SIDE),
        compiler_params=pltpu.CompilerParams(vmem_limit_bytes=VMEM_BYTES),
        cost_estimate=pl.CostEstimate(
            flops=2 * SIDE * count * rows * depth,
            bytes_accessed=2 * (rows + SIDE * count) * depth,
            transcendentals=0,
        ),
    )(slot, features, down, up)


QUAD = 4


def lanes_of(rows, rank, swapped):
    row = lax.broadcasted_iota(jnp.int32, (rows, 2 * rank), 0)
    lane = lax.broadcasted_iota(jnp.int32, (rows, 2 * rank), 1)
    member = (row % 16) // QUAD
    half = (lane // rank) ^ swapped
    return (member % 2) == half, member < 2


def shrink_kernel(s0, s1, s2, s3, own_ref, other_ref, o_ref):
    rank = o_ref.shape[1] // 2
    nt = (((1,), (1,)), ((), ()))
    quads = own_ref.shape[0] // (QUAD * rank)
    for pair in range(quads):
        total = None
        for swapped, weight_ref in ((0, own_ref), (1, other_ref)):
            quad = pair + swapped * quads
            rows = jnp.concatenate([s[quad * 16 : (quad + 1) * 16, :] for s in (s0, s1, s2, s3)])
            weight = weight_ref[pair * QUAD * rank : (pair + 1) * QUAD * rank, :]
            if swapped:
                weight = jnp.concatenate(
                    [weight[(m ^ 1) * rank : ((m ^ 1) + 1) * rank] for m in range(QUAD)]
                )
            got = lax.dot_general(rows, weight, nt, preferred_element_type=F32)
            mine, first = lanes_of(rows.shape[0], rank, swapped)
            kept = jnp.where(first, got[:, : 2 * rank], got[:, 2 * rank :])
            kept = jnp.where(mine, kept, 0.0)
            total = kept if total is None else total + kept
        o_ref[pair * 64 : (pair + 1) * 64, :] = total.astype(BF16)


def shrink(slots, own, other):
    rank = 64
    return pl.pallas_call(
        shrink_kernel,
        name="shrink",
        out_shape=jax.ShapeDtypeStruct((own.shape[0] // (QUAD * rank) * 64, 2 * rank), BF16),
        in_specs=whole(6),
        out_specs=whole(1)[0],
        compiler_params=pltpu.CompilerParams(vmem_limit_bytes=VMEM_BYTES),
        cost_estimate=pl.CostEstimate(flops=2**28, bytes_accessed=2**22, transcendentals=0),
    )(*slots, own, other)


def grow_kernel(h_ref, own_ref, other_ref, *outs):
    rank = h_ref.shape[1] // 2
    quads = own_ref.shape[0] // (QUAD * rank)
    for pair in range(quads):
        held = h_ref[pair * 64 : (pair + 1) * 64, :].astype(F32)
        for swapped, weight_ref in ((0, own_ref), (1, other_ref)):
            quad = pair + swapped * quads
            weight = weight_ref[pair * QUAD * rank : (pair + 1) * QUAD * rank, :]
            if swapped:
                weight = jnp.concatenate(
                    [weight[(m ^ 1) * rank : ((m ^ 1) + 1) * rank] for m in range(QUAD)]
                )
            mine, first = lanes_of(held.shape[0], rank, swapped)
            left = jnp.where(mine & first, held, 0.0).astype(BF16)
            right = jnp.where(mine & ~first, held, 0.0).astype(BF16)
            got = jnp.dot(
                jnp.concatenate([left, right], axis=1), weight, preferred_element_type=F32
            ).astype(BF16)
            for k in range(SIDE):
                outs[k][quad * 16 : (quad + 1) * 16, :] = got[k * 16 : (k + 1) * 16]


def grow(shrunk, own, other, count):
    return pl.pallas_call(
        grow_kernel,
        name="grow",
        out_shape=[jax.ShapeDtypeStruct((count, own.shape[1]), BF16)] * SIDE,
        in_specs=whole(3),
        out_specs=whole(SIDE),
        compiler_params=pltpu.CompilerParams(vmem_limit_bytes=VMEM_BYTES),
        cost_estimate=pl.CostEstimate(flops=2**28, bytes_accessed=2**22, transcendentals=0),
    )(shrunk, own, other)


def collect_kernel(slot_ref, r0, r1, r2, r3, o_ref):
    count = r0.shape[0]
    blocks, rows, cols = o_ref.shape
    total = jnp.zeros((blocks * rows, cols), F32)
    for k, ref in enumerate((r0, r1, r2, r3)):
        slots = lax.broadcasted_iota(jnp.int32, (count, blocks * rows), 0) + k * count
        placing = (slots == slot_ref[...]).astype(F32).astype(BF16)
        total = total + lax.dot_general(
            placing, ref[...], (((0,), (0,)), ((), ())), preferred_element_type=F32
        )
    for t in range(blocks):
        o_ref[t] = total[t * rows : (t + 1) * rows].astype(BF16)


def collect(slot, returned, blocks):
    rows = slot.shape[1]
    cols = returned[0].shape[1]
    return pl.pallas_call(
        collect_kernel,
        name="collect",
        out_shape=jax.ShapeDtypeStruct((blocks, rows // blocks, cols), BF16),
        in_specs=whole(5),
        out_specs=whole(1)[0],
        compiler_params=pltpu.CompilerParams(vmem_limit_bytes=VMEM_BYTES),
        cost_estimate=pl.CostEstimate(flops=2**28, bytes_accessed=2**21, transcendentals=0),
    )(slot, *returned)


def finish_kernel(skip_ref, s_ref, a_ref, b_ref, c_ref, delta_ref, o_ref):
    blocks, _, cols = delta_ref.shape
    for t in range(blocks):
        at = slice(t * cols, (t + 1) * cols)
        base = (
            s_ref[:, at].astype(F32)
            + a_ref[:, at].astype(F32)
            + b_ref[:, at].astype(F32)
            + c_ref[:, at].astype(F32)
        )
        o_ref[:, at] = (
            skip_ref[:, at].astype(F32) + base + 2.0 * delta_ref[t].astype(F32)
        ).astype(BF16)


def finish(*operands):
    rows_of = operands[0].shape
    return pl.pallas_call(
        finish_kernel,
        name="finish",
        out_shape=jax.ShapeDtypeStruct(operands[0].shape, BF16),
        grid=(1,),
        in_specs=[
            pl.BlockSpec(rows_of, lambda i: (0, 0)),
            pl.BlockSpec(rows_of, lambda i: (0, 0)),
            pl.BlockSpec(rows_of, lambda i: (0, 0)),
            pl.BlockSpec(rows_of, lambda i: (0, 0)),
            pl.BlockSpec(rows_of, lambda i: (0, 0)),
            pl.BlockSpec(operands[5].shape, lambda i: (0, 0, 0)),
        ],
        out_specs=pl.BlockSpec(rows_of, lambda i: (0, 0)),
        compiler_params=pltpu.CompilerParams(vmem_limit_bytes=VMEM_BYTES),
        cost_estimate=pl.CostEstimate(flops=2**20, bytes_accessed=2**21, transcendentals=0),
    )(*operands)


def wide_sum(*terms):
    return sum(term.astype(F32) for term in terms)


def body(
    queries,
    cached_key_rows,
    cached_value_rows,
    fresh_key,
    fresh_value,
    lengths,
    adapter_index,
    skip_stream,
    output_weight,
    adapter_down_weight,
    adapter_up_weight,
):
    blocks = lax.axis_size("tp")
    rep, tp = lax.axis_index("rep"), lax.axis_index("tp")
    held, depth, rank = adapter_down_weight.shape
    width = output_weight.shape[1]

    down_own = jnp.swapaxes(adapter_down_weight, 1, 2).reshape(held * rank, depth)
    up_own = adapter_up_weight.reshape(held * rank, depth)
    down_other = pass_core(down_own)
    up_other = pass_core(up_own)

    adapter = adapter_index[:, 0]
    rows = adapter.shape[0]
    same = adapter[:, None] == adapter[None, :]
    count_up = jnp.arange(rows, dtype=jnp.int32)
    ranked = jnp.sum((same & (count_up[:, None] > count_up[None, :])).astype(jnp.int32), axis=1)
    owner = adapter // held
    cap = 4
    per_z = 2 * held * cap
    slot = (
        (owner // 2 - rep // 2) % SIDE * per_z
        + ((owner % 2) ^ (rep % 2)) * (held * cap)
        + (adapter % held) * cap
        + ranked
    ).reshape(1, rows)
    order = lax.dynamic_slice(jnp.asarray(row_order()), (rep * blocks + tp, 0), (1, blocks))[0]

    attended = attend(
        queries, cached_key_rows, cached_value_rows, fresh_key, fresh_value, lengths, blocks
    )
    features = lax.all_to_all(attended, "tp", split_axis=0, concat_axis=0, tiled=True)
    flat = features.reshape(rows, depth)

    placed = dispatch(slot, flat, per_z, down_other, up_other)
    arrived = [placed[0]] + [pass_z(placed[k], k) for k in range(1, SIDE)]

    own, ahead, back, ahead_last, back_last = project(order, features, output_weight)
    ahead, *arrived = lax.optimization_barrier((ahead, *arrived))
    came_ahead, came_back = pass_plane(ahead, "xy", 1), pass_plane(back, "xy", -1)

    shrunk = shrink(arrived, down_own, down_other)
    near = [pass_plane(shrunk, "yx", k) for k in range(1, SIDE)]
    shrunk = wide_sum(shrunk, *near).astype(BF16)
    near = [pass_plane(shrunk, "xy", k) for k in range(1, SIDE)]
    ahead_last, back_last = meet(ahead_last, back_last, came_ahead, came_back)
    *near, ahead_last, back_last = lax.optimization_barrier((*near, ahead_last, back_last))
    shrunk = wide_sum(shrunk, *near).astype(BF16)
    ahead_last, back_last = pass_plane(ahead_last, "xy", 1), pass_plane(back_last, "xy", -1)
    grown = grow(shrunk, up_own, up_other, per_z)
    returned = [grown[0]] + [pass_z(grown[k], -k) for k in range(1, SIDE)]
    returned[1], returned[2], back_last = lax.optimization_barrier((returned[1], returned[2], back_last))
    summed = join(own, came_ahead, came_back, ahead_last, back_last)
    delta = collect(slot, returned, blocks)

    second = [pass_plane(summed[k], "yx", k) for k in range(1, SIDE)]
    delta = lax.all_to_all(delta, "tp", split_axis=0, concat_axis=0, tiled=True)
    return finish(skip_stream, summed[0], *second, delta)


def solution(mesh):
    return jax.shard_map(
        body,
        mesh=mesh,
        in_specs=(
            P(BOTH, None, None),
            P(BOTH, None, None, None),
            P(BOTH, None, None, None),
            P(BOTH, None, None),
            P(BOTH, None, None),
            P(BOTH),
            P("rep", None),
            P(BOTH, None),
            P("tp", None),
            P("rep", "tp", None),
            P("rep", None, "tp"),
        ),
        out_specs=P(BOTH, None),
        check_vma=False,
    )
```

```python
import math

import jax
import jax.numpy as jnp
import numpy as np
from jax import lax
from jax.experimental import pallas as pl
from jax.experimental.pallas import tpu as pltpu
from jax.sharding import PartitionSpec as P

F32 = jnp.float32
BF16 = jnp.bfloat16
BOTH = ("rep", "tp")
SIDE = 4
VMEM_BYTES = 24 * 1024 * 1024
FULL_VMEM = 60 * 1024 * 1024


def place(z, c, y, x):
    return ((z * 2 + c) * SIDE + y) * SIDE + x


PLACES = [
    (z, c, y, x) for z in range(SIDE) for c in range(2) for y in range(SIDE) for x in range(SIDE)
]


def pass_plane(value, axis_of_core, offset):
    pairs = []
    for z, c, y, x in PLACES:
        if axis_of_core[c] == "x":
            to = place(z, c, y, (x + offset) % SIDE)
        else:
            to = place(z, c, (y + offset) % SIDE, x)
        pairs.append((place(z, c, y, x), to))
    return lax.ppermute(value, BOTH, pairs)


def pass_z(value, offset):
    pairs = [(place(z, c, y, x), place((z + offset) % SIDE, c, y, x)) for z, c, y, x in PLACES]
    return lax.ppermute(value, BOTH, pairs)


def pass_core(value):
    return lax.ppermute(
        value, BOTH, [(place(z, c, y, x), place(z, 1 - c, y, x)) for z, c, y, x in PLACES]
    )


def row_order():
    table = np.zeros((len(PLACES), SIDE * SIDE), np.int32)
    for z, c, y, x in PLACES:
        for first in range(SIDE):
            for second in range(SIDE):
                dx, dy = (first, second) if c == 0 else (second, first)
                table[place(z, c, y, x), first * SIDE + second] = (
                    (y + dy) % SIDE * SIDE + (x + dx) % SIDE
                )
    return table


AT_ONCE = 4


def attend_kernel(
    lengths_ref, q_ref, k_hbm, v_hbm, fk_ref, fv_ref, o_ref, k_ref, v_ref, mixed_ref, k_sem, v_sem
):
    rows, heads, width = q_ref.shape
    groups, span = k_ref.shape[1], k_ref.shape[2]
    fold = heads // groups
    steps = rows // AT_ONCE
    factor = 1.0 / math.sqrt(width)
    nt = (((1,), (1,)), ((), ()))

    def copy(step, far, near, sem):
        at = pl.ds(step * AT_ONCE, AT_ONCE)
        return pltpu.make_async_copy(far.at[at], near.at[at], sem.at[step])

    for step in range(steps - 1):
        copy(step, k_hbm, k_ref, k_sem).start()
        copy(step, v_hbm, v_ref, v_sem).start()

    def one_step(step, carry):
        copy(step, k_hbm, k_ref, k_sem).wait()

        @pl.when(step == 0)
        def _():
            copy(steps - 1, k_hbm, k_ref, k_sem).start()
            copy(steps - 1, v_hbm, v_ref, v_sem).start()

        all_scores = []
        for item in range(AT_ONCE):
            row = step * AT_ONCE + item
            q = q_ref[row]
            parts = []
            for g in range(groups):
                two = q[(g // 2) * 2 * fold : (g // 2 + 1) * 2 * fold]
                got = lax.dot_general(two, k_ref[row, g], nt, preferred_element_type=F32)
                parts.append(got[(g % 2) * fold : (g % 2 + 1) * fold])
            all_scores.append(jnp.concatenate(parts, axis=0) * factor)
        copy(step, v_hbm, v_ref, v_sem).wait()
        for item in range(AT_ONCE):
            row = step * AT_ONCE + item
            scores = all_scores[item]
            fresh_k = jnp.broadcast_to(
                fk_ref[row].astype(F32)[:, None, :], (groups, fold, width)
            ).reshape(heads, width)
            own = jnp.sum(q_ref[row].astype(F32) * fresh_k, axis=-1, keepdims=True) * factor
            position = lax.broadcasted_iota(jnp.int32, (heads, span), 1)
            masked = jnp.where(position < lengths_ref[row], scores, -jnp.inf)
            top = jnp.maximum(jnp.max(masked, axis=-1, keepdims=True), own)
            expo = jnp.exp(masked - top)
            expo_own = jnp.exp(own - top)
            inverse = 1.0 / (jnp.sum(expo, axis=-1, keepdims=True) + expo_own)
            probs = (expo * inverse).astype(BF16)
            probs_own = (expo_own * inverse).astype(BF16).astype(F32)
            parts = []
            for g in range(groups):
                two = probs[(g // 2) * 2 * fold : (g // 2 + 1) * 2 * fold]
                got = jnp.dot(two, v_ref[row, g], preferred_element_type=F32)
                parts.append(got[(g % 2) * fold : (g % 2 + 1) * fold])
            fresh_v = jnp.broadcast_to(
                fv_ref[row].astype(F32)[:, None, :], (groups, fold, width)
            ).reshape(heads, width)
            mixed = jnp.concatenate(parts, axis=0) + probs_own * fresh_v
            mixed_ref[pl.ds(pl.multiple_of(row * heads, heads), heads), :] = mixed
        return carry

    lax.fori_loop(0, steps, one_step, 0)
    per_block = o_ref.shape[2] // width
    for h in range(heads):
        tile = jnp.concatenate(
            [
                mixed_ref[pl.ds(half * 8 * heads + h, 8, stride=heads), :]
                for half in range(rows // 8)
            ],
            axis=0,
        )
        lane = (h % per_block) * width
        o_ref[h // per_block, :, lane : lane + width] = tile.astype(BF16)


def attend(queries, keys, values, fresh_key, fresh_value, lengths, blocks):
    rows, heads, width = queries.shape
    vmem = pl.BlockSpec(memory_space=pltpu.VMEM)
    far = pl.BlockSpec(memory_space=pl.ANY)
    return pl.pallas_call(
        attend_kernel,
        name="attend",
        out_shape=jax.ShapeDtypeStruct((blocks, rows, heads * width // blocks), BF16),
        in_specs=[pl.BlockSpec(memory_space=pltpu.SMEM), vmem, far, far, vmem, vmem],
        out_specs=vmem,
        scratch_shapes=[
            pltpu.VMEM(keys.shape, BF16),
            pltpu.VMEM(values.shape, BF16),
            pltpu.VMEM((rows * heads, width), F32),
            pltpu.SemaphoreType.DMA((rows // AT_ONCE,)),
            pltpu.SemaphoreType.DMA((rows // AT_ONCE,)),
        ],
        compiler_params=pltpu.CompilerParams(vmem_limit_bytes=FULL_VMEM),
        cost_estimate=pl.CostEstimate(
            flops=4 * keys.size * heads // keys.shape[1],
            bytes_accessed=4 * keys.size,
            transcendentals=0,
        ),
    )(lengths, queries, keys, values, fresh_key, fresh_value)


def whole(count):
    return [pl.BlockSpec(memory_space=pltpu.VMEM)] * count


TILES = 4


def project_kernel(order_ref, f_ref, w_hbm, own, ahead, back, ahead_last, back_last, *scratch):
    rows_ref, w_ref, out_ref, w_sem, o_sem = scratch
    block = f_ref.shape[1]
    tile = w_ref.shape[2]
    chunk = rows_ref.shape[0] // SIDE
    half = TILES // 2

    def arrival(k):
        return pltpu.make_async_copy(w_hbm.at[:, pl.ds(k * tile, tile)], w_ref.at[k], w_sem.at[k])

    def departure(k, part):
        low = k < half
        to = (
            own,
            ahead_last if low else ahead,
            ahead if low else back,
            back if low else back_last,
        )[part]
        column = (k if to.shape[1] == tile * TILES else k % half) * tile
        return pltpu.make_async_copy(
            out_ref.at[k, pl.ds(part * chunk, chunk)],
            to.at[:, pl.ds(column, tile)],
            o_sem.at[k, part],
        )

    for k in range(TILES):
        arrival(k).start()
    for k in range(SIDE * SIDE):
        rows_ref[k * block : (k + 1) * block, :] = f_ref[order_ref[k]]
    for k in range(TILES):
        arrival(k).wait()
        out_ref[k] = jnp.dot(rows_ref[...], w_ref[k], preferred_element_type=F32).astype(BF16)
        for part in range(SIDE):
            departure(k, part).start()
    for k in range(TILES):
        for part in range(SIDE):
            departure(k, part).wait()


def project(order, features, weight):
    blocks, rows, depth = features.shape
    cols = weight.shape[1]
    tile = cols // TILES
    chunk = blocks * rows // SIDE
    far = pl.BlockSpec(memory_space=pl.ANY)
    full = jax.ShapeDtypeStruct((chunk, cols), BF16)
    part = jax.ShapeDtypeStruct((chunk, cols // 2), BF16)
    return pl.pallas_call(
        project_kernel,
        name="project",
        out_shape=[full, full, full, part, part],
        in_specs=[
            pl.BlockSpec(memory_space=pltpu.SMEM),
            pl.BlockSpec(memory_space=pltpu.VMEM),
            far,
        ],
        out_specs=[far] * 5,
        scratch_shapes=[
            pltpu.VMEM((blocks * rows, depth), BF16),
            pltpu.VMEM((TILES, depth, tile), BF16),
            pltpu.VMEM((TILES, blocks * rows, tile), BF16),
            pltpu.SemaphoreType.DMA((TILES,)),
            pltpu.SemaphoreType.DMA((TILES, SIDE)),
        ],
        compiler_params=pltpu.CompilerParams(vmem_limit_bytes=56 * 1024 * 1024),
        cost_estimate=pl.CostEstimate(
            flops=2 * blocks * rows * depth * cols,
            bytes_accessed=2 * depth * cols + 2 * blocks * rows * cols,
            transcendentals=0,
        ),
    )(order, features, weight)


def meet_kernel(last, came, o_ref, *, first):
    came_half = came[:, first : first + o_ref.shape[1]]
    o_ref[...] = (last[...].astype(F32) + came_half.astype(F32)).astype(BF16)


def meet(last, came, first):
    return pl.pallas_call(
        lambda *refs: meet_kernel(*refs, first=first),
        name="meet",
        out_shape=jax.ShapeDtypeStruct(last.shape, BF16),
        in_specs=whole(2),
        out_specs=whole(1)[0],
        compiler_params=pltpu.CompilerParams(vmem_limit_bytes=VMEM_BYTES),
        cost_estimate=pl.CostEstimate(flops=2**20, bytes_accessed=2**22, transcendentals=0),
    )(last, came)


def join_kernel(own, came_ahead, came_back, ahead_last, back_last, *outs):
    rows = outs[0].shape[0]
    half = ahead_last.shape[1]
    for k in range(SIDE):
        at = slice(k * rows, (k + 1) * rows)
        for right in range(2):
            cols = slice(right * half, (right + 1) * half)
            total = own[at, cols].astype(F32)
            if right:
                total = total + came_ahead[at, cols].astype(F32) + back_last[at].astype(F32)
            else:
                total = total + ahead_last[at].astype(F32) + came_back[at, cols].astype(F32)
            outs[k][:, cols] = total.astype(BF16)


def join(*operands):
    rows, cols = operands[0].shape
    return pl.pallas_call(
        join_kernel,
        name="join",
        out_shape=[jax.ShapeDtypeStruct((rows // SIDE, cols), BF16)] * SIDE,
        in_specs=whole(5),
        out_specs=whole(SIDE),
        compiler_params=pltpu.CompilerParams(vmem_limit_bytes=VMEM_BYTES),
        cost_estimate=pl.CostEstimate(flops=2**20, bytes_accessed=2**22, transcendentals=0),
    )(*operands)


def dispatch_kernel(slot_ref, f_ref, _down, _up, *outs):
    count = outs[0].shape[0]
    rows = f_ref.shape[0]
    features = f_ref[...]
    for k in range(SIDE):
        slots = lax.broadcasted_iota(jnp.int32, (count, rows), 0) + k * count
        placing = (slots == slot_ref[...]).astype(F32).astype(BF16)
        outs[k][...] = jnp.dot(placing, features, preferred_element_type=F32).astype(BF16)


def dispatch(slot, features, count, down, up):
    rows, depth = features.shape
    return pl.pallas_call(
        dispatch_kernel,
        name="dispatch",
        out_shape=[jax.ShapeDtypeStruct((count, depth), BF16)] * SIDE,
        in_specs=whole(2) + [pl.BlockSpec(memory_space=pl.ANY)] * 2,
        out_specs=whole(SIDE),
        compiler_params=pltpu.CompilerParams(vmem_limit_bytes=VMEM_BYTES),
        cost_estimate=pl.CostEstimate(
            flops=2 * SIDE * count * rows * depth,
            bytes_accessed=2 * (rows + SIDE * count) * depth,
            transcendentals=0,
        ),
    )(slot, features, down, up)


QUAD = 4


def lanes_of(rows, rank, swapped):
    row = lax.broadcasted_iota(jnp.int32, (rows, 2 * rank), 0)
    lane = lax.broadcasted_iota(jnp.int32, (rows, 2 * rank), 1)
    member = (row % 16) // QUAD
    half = (lane // rank) ^ swapped
    return (member % 2) == half, member < 2


def shrink_kernel(s0, s1, s2, s3, own_ref, other_ref, o_ref):
    rank = o_ref.shape[1] // 2
    nt = (((1,), (1,)), ((), ()))
    quads = own_ref.shape[0] // (QUAD * rank)
    for pair in range(quads):
        total = None
        for swapped, weight_ref in ((0, own_ref), (1, other_ref)):
            quad = pair + swapped * quads
            rows = jnp.concatenate([s[quad * 16 : (quad + 1) * 16, :] for s in (s0, s1, s2, s3)])
            weight = weight_ref[pair * QUAD * rank : (pair + 1) * QUAD * rank, :]
            if swapped:
                weight = jnp.concatenate(
                    [weight[(m ^ 1) * rank : ((m ^ 1) + 1) * rank] for m in range(QUAD)]
                )
            got = lax.dot_general(rows, weight, nt, preferred_element_type=F32)
            mine, first = lanes_of(rows.shape[0], rank, swapped)
            kept = jnp.where(first, got[:, : 2 * rank], got[:, 2 * rank :])
            kept = jnp.where(mine, kept, 0.0)
            total = kept if total is None else total + kept
        o_ref[pair * 64 : (pair + 1) * 64, :] = total.astype(BF16)


def shrink(slots, own, other):
    rank = 64
    return pl.pallas_call(
        shrink_kernel,
        name="shrink",
        out_shape=jax.ShapeDtypeStruct((own.shape[0] // (QUAD * rank) * 64, 2 * rank), BF16),
        in_specs=whole(6),
        out_specs=whole(1)[0],
        compiler_params=pltpu.CompilerParams(vmem_limit_bytes=VMEM_BYTES),
        cost_estimate=pl.CostEstimate(flops=2**28, bytes_accessed=2**22, transcendentals=0),
    )(*slots, own, other)


def grow_kernel(h_ref, own_ref, other_ref, *outs):
    rank = h_ref.shape[1] // 2
    quads = own_ref.shape[0] // (QUAD * rank)
    for pair in range(quads):
        held = h_ref[pair * 64 : (pair + 1) * 64, :].astype(F32)
        for swapped, weight_ref in ((0, own_ref), (1, other_ref)):
            quad = pair + swapped * quads
            weight = weight_ref[pair * QUAD * rank : (pair + 1) * QUAD * rank, :]
            if swapped:
                weight = jnp.concatenate(
                    [weight[(m ^ 1) * rank : ((m ^ 1) + 1) * rank] for m in range(QUAD)]
                )
            mine, first = lanes_of(held.shape[0], rank, swapped)
            left = jnp.where(mine & first, held, 0.0).astype(BF16)
            right = jnp.where(mine & ~first, held, 0.0).astype(BF16)
            got = jnp.dot(
                jnp.concatenate([left, right], axis=1), weight, preferred_element_type=F32
            ).astype(BF16)
            for k in range(SIDE):
                outs[k][quad * 16 : (quad + 1) * 16, :] = got[k * 16 : (k + 1) * 16]


def grow(shrunk, own, other, count):
    return pl.pallas_call(
        grow_kernel,
        name="grow",
        out_shape=[jax.ShapeDtypeStruct((count, own.shape[1]), BF16)] * SIDE,
        in_specs=whole(3),
        out_specs=whole(SIDE),
        compiler_params=pltpu.CompilerParams(vmem_limit_bytes=VMEM_BYTES),
        cost_estimate=pl.CostEstimate(flops=2**28, bytes_accessed=2**22, transcendentals=0),
    )(shrunk, own, other)


def collect_kernel(slot_ref, r0, r1, r2, r3, o_ref):
    count = r0.shape[0]
    blocks, rows, cols = o_ref.shape
    total = jnp.zeros((blocks * rows, cols), F32)
    for k, ref in enumerate((r0, r1, r2, r3)):
        slots = lax.broadcasted_iota(jnp.int32, (count, blocks * rows), 0) + k * count
        placing = (slots == slot_ref[...]).astype(F32).astype(BF16)
        total = total + lax.dot_general(
            placing, ref[...], (((0,), (0,)), ((), ())), preferred_element_type=F32
        )
    for t in range(blocks):
        o_ref[t] = total[t * rows : (t + 1) * rows].astype(BF16)


def collect(slot, returned, blocks):
    rows = slot.shape[1]
    cols = returned[0].shape[1]
    return pl.pallas_call(
        collect_kernel,
        name="collect",
        out_shape=jax.ShapeDtypeStruct((blocks, rows // blocks, cols), BF16),
        in_specs=whole(5),
        out_specs=whole(1)[0],
        compiler_params=pltpu.CompilerParams(vmem_limit_bytes=VMEM_BYTES),
        cost_estimate=pl.CostEstimate(flops=2**28, bytes_accessed=2**21, transcendentals=0),
    )(slot, *returned)


def finish_kernel(skip_ref, s_ref, a_ref, b_ref, c_ref, delta_ref, o_ref):
    blocks, _, cols = delta_ref.shape
    for t in range(blocks):
        at = slice(t * cols, (t + 1) * cols)
        base = (
            s_ref[:, at].astype(F32)
            + a_ref[:, at].astype(F32)
            + b_ref[:, at].astype(F32)
            + c_ref[:, at].astype(F32)
        )
        o_ref[:, at] = (
            skip_ref[:, at].astype(F32) + base + 2.0 * delta_ref[t].astype(F32)
        ).astype(BF16)


def finish(*operands):
    rows_of = operands[0].shape
    return pl.pallas_call(
        finish_kernel,
        name="finish",
        out_shape=jax.ShapeDtypeStruct(operands[0].shape, BF16),
        grid=(1,),
        in_specs=[
            pl.BlockSpec(rows_of, lambda i: (0, 0)),
            pl.BlockSpec(rows_of, lambda i: (0, 0)),
            pl.BlockSpec(rows_of, lambda i: (0, 0)),
            pl.BlockSpec(rows_of, lambda i: (0, 0)),
            pl.BlockSpec(rows_of, lambda i: (0, 0)),
            pl.BlockSpec(operands[5].shape, lambda i: (0, 0, 0)),
        ],
        out_specs=pl.BlockSpec(rows_of, lambda i: (0, 0)),
        compiler_params=pltpu.CompilerParams(vmem_limit_bytes=VMEM_BYTES),
        cost_estimate=pl.CostEstimate(flops=2**20, bytes_accessed=2**21, transcendentals=0),
    )(*operands)


def wide_sum(*terms):
    return sum(term.astype(F32) for term in terms)


def body(
    queries,
    cached_key_rows,
    cached_value_rows,
    fresh_key,
    fresh_value,
    lengths,
    adapter_index,
    skip_stream,
    output_weight,
    adapter_down_weight,
    adapter_up_weight,
):
    blocks = lax.axis_size("tp")
    rep, tp = lax.axis_index("rep"), lax.axis_index("tp")
    held, depth, rank = adapter_down_weight.shape
    width = output_weight.shape[1]

    down_own = jnp.swapaxes(adapter_down_weight, 1, 2).reshape(held * rank, depth)
    up_own = adapter_up_weight.reshape(held * rank, depth)
    down_other = pass_core(down_own)
    up_other = pass_core(up_own)

    adapter = adapter_index[:, 0]
    rows = adapter.shape[0]
    same = adapter[:, None] == adapter[None, :]
    count_up = jnp.arange(rows, dtype=jnp.int32)
    ranked = jnp.sum((same & (count_up[:, None] > count_up[None, :])).astype(jnp.int32), axis=1)
    owner = adapter // held
    cap = 4
    per_z = 2 * held * cap
    slot = (
        (owner // 2 - rep // 2) % SIDE * per_z
        + ((owner % 2) ^ (rep % 2)) * (held * cap)
        + (adapter % held) * cap
        + ranked
    ).reshape(1, rows)
    order = lax.dynamic_slice(jnp.asarray(row_order()), (rep * blocks + tp, 0), (1, blocks))[0]

    attended = attend(
        queries, cached_key_rows, cached_value_rows, fresh_key, fresh_value, lengths, blocks
    )
    features = lax.all_to_all(attended, "tp", split_axis=0, concat_axis=0, tiled=True)
    flat = features.reshape(rows, depth)

    placed = dispatch(slot, flat, per_z, down_other, up_other)
    arrived = [placed[0]] + [pass_z(placed[k], k) for k in range(1, SIDE)]

    own, ahead, back, ahead_last, back_last = project(order, features, output_weight)
    ahead, *arrived = lax.optimization_barrier((ahead, *arrived))
    came_ahead, came_back = pass_plane(ahead, "xy", 1), pass_plane(back, "xy", -1)

    shrunk = shrink(arrived, down_own, down_other)
    near = [pass_plane(shrunk, "yx", k) for k in range(1, SIDE)]
    shrunk = wide_sum(shrunk, *near).astype(BF16)
    near = [pass_plane(shrunk, "xy", k) for k in range(1, SIDE)]
    back_last = meet(back_last, came_back, back_last.shape[1])
    ahead_last = meet(ahead_last, came_ahead, 0)
    *near, ahead_last = lax.optimization_barrier((*near, ahead_last))
    shrunk = wide_sum(shrunk, *near).astype(BF16)
    ahead_last, back_last = pass_plane(ahead_last, "xy", 1), pass_plane(back_last, "xy", -1)
    grown = grow(shrunk, up_own, up_other, per_z)
    returned = [grown[0]] + [pass_z(grown[k], -k) for k in range(1, SIDE)]
    returned[1], returned[2], back_last = lax.optimization_barrier((returned[1], returned[2], back_last))
    summed = join(own, came_ahead, came_back, ahead_last, back_last)
    delta = collect(slot, returned, blocks)

    second = [pass_plane(summed[k], "yx", k) for k in range(1, SIDE)]
    delta = lax.all_to_all(delta, "tp", split_axis=0, concat_axis=0, tiled=True)
    return finish(skip_stream, summed[0], *second, delta)


def solution(mesh):
    return jax.shard_map(
        body,
        mesh=mesh,
        in_specs=(
            P(BOTH, None, None),
            P(BOTH, None, None, None),
            P(BOTH, None, None, None),
            P(BOTH, None, None),
            P(BOTH, None, None),
            P(BOTH),
            P("rep", None),
            P(BOTH, None),
            P("tp", None),
            P("rep", "tp", None),
            P("rep", None, "tp"),
        ),
        out_specs=P(BOTH, None),
        check_vma=False,
    )
```

```python
import math

import jax
import jax.numpy as jnp
import numpy as np
from jax import lax
from jax.experimental import pallas as pl
from jax.experimental.pallas import tpu as pltpu
from jax.sharding import PartitionSpec as P

F32 = jnp.float32
BF16 = jnp.bfloat16
BOTH = ("rep", "tp")
SIDE = 4
VMEM_BYTES = 24 * 1024 * 1024
FULL_VMEM = 60 * 1024 * 1024


def place(z, c, y, x):
    return ((z * 2 + c) * SIDE + y) * SIDE + x


PLACES = [
    (z, c, y, x) for z in range(SIDE) for c in range(2) for y in range(SIDE) for x in range(SIDE)
]


def pass_plane(value, axis_of_core, offset):
    pairs = []
    for z, c, y, x in PLACES:
        if axis_of_core[c] == "x":
            to = place(z, c, y, (x + offset) % SIDE)
        else:
            to = place(z, c, (y + offset) % SIDE, x)
        pairs.append((place(z, c, y, x), to))
    return lax.ppermute(value, BOTH, pairs)


def pass_z(value, offset):
    pairs = [(place(z, c, y, x), place((z + offset) % SIDE, c, y, x)) for z, c, y, x in PLACES]
    return lax.ppermute(value, BOTH, pairs)


def pass_core(value):
    return lax.ppermute(
        value, BOTH, [(place(z, c, y, x), place(z, 1 - c, y, x)) for z, c, y, x in PLACES]
    )


def row_order():
    table = np.zeros((len(PLACES), SIDE * SIDE), np.int32)
    for z, c, y, x in PLACES:
        for first in range(SIDE):
            for second in range(SIDE):
                dx, dy = (first, second) if c == 0 else (second, first)
                table[place(z, c, y, x), first * SIDE + second] = (
                    (y + dy) % SIDE * SIDE + (x + dx) % SIDE
                )
    return table


AT_ONCE = 4


def attend_kernel(
    lengths_ref, q_ref, k_hbm, v_hbm, fk_ref, fv_ref, o_ref, k_ref, v_ref, mixed_ref, k_sem, v_sem
):
    rows, heads, width = q_ref.shape
    groups, span = k_ref.shape[1], k_ref.shape[2]
    fold = heads // groups
    steps = rows // AT_ONCE
    factor = 1.0 / math.sqrt(width)
    nt = (((1,), (1,)), ((), ()))

    def copy(step, far, near, sem):
        at = pl.ds(step * AT_ONCE, AT_ONCE)
        return pltpu.make_async_copy(far.at[at], near.at[at], sem.at[step])

    for step in range(steps - 1):
        copy(step, k_hbm, k_ref, k_sem).start()
        copy(step, v_hbm, v_ref, v_sem).start()

    def one_step(step, carry):
        copy(step, k_hbm, k_ref, k_sem).wait()

        @pl.when(step == 0)
        def _():
            copy(steps - 1, k_hbm, k_ref, k_sem).start()
            copy(steps - 1, v_hbm, v_ref, v_sem).start()

        all_scores = []
        for item in range(AT_ONCE):
            row = step * AT_ONCE + item
            q = q_ref[row]
            parts = []
            for g in range(groups):
                two = q[(g // 2) * 2 * fold : (g // 2 + 1) * 2 * fold]
                got = lax.dot_general(two, k_ref[row, g], nt, preferred_element_type=F32)
                parts.append(got[(g % 2) * fold : (g % 2 + 1) * fold])
            all_scores.append(jnp.concatenate(parts, axis=0) * factor)
        copy(step, v_hbm, v_ref, v_sem).wait()
        for item in range(AT_ONCE):
            row = step * AT_ONCE + item
            scores = all_scores[item]
            fresh_k = jnp.broadcast_to(
                fk_ref[row].astype(F32)[:, None, :], (groups, fold, width)
            ).reshape(heads, width)
            own = jnp.sum(q_ref[row].astype(F32) * fresh_k, axis=-1, keepdims=True) * factor
            position = lax.broadcasted_iota(jnp.int32, (heads, span), 1)
            masked = jnp.where(position < lengths_ref[row], scores, -jnp.inf)
            top = jnp.maximum(jnp.max(masked, axis=-1, keepdims=True), own)
            expo = jnp.exp(masked - top)
            expo_own = jnp.exp(own - top)
            inverse = 1.0 / (jnp.sum(expo, axis=-1, keepdims=True) + expo_own)
            probs = (expo * inverse).astype(BF16)
            probs_own = (expo_own * inverse).astype(BF16).astype(F32)
            parts = []
            for g in range(groups):
                two = probs[(g // 2) * 2 * fold : (g // 2 + 1) * 2 * fold]
                got = jnp.dot(two, v_ref[row, g], preferred_element_type=F32)
                parts.append(got[(g % 2) * fold : (g % 2 + 1) * fold])
            fresh_v = jnp.broadcast_to(
                fv_ref[row].astype(F32)[:, None, :], (groups, fold, width)
            ).reshape(heads, width)
            mixed = jnp.concatenate(parts, axis=0) + probs_own * fresh_v
            mixed_ref[pl.ds(pl.multiple_of(row * heads, heads), heads), :] = mixed
        return carry

    lax.fori_loop(0, steps, one_step, 0)
    per_block = o_ref.shape[2] // width
    for h in range(heads):
        tile = jnp.concatenate(
            [
                mixed_ref[pl.ds(half * 8 * heads + h, 8, stride=heads), :]
                for half in range(rows // 8)
            ],
            axis=0,
        )
        lane = (h % per_block) * width
        o_ref[h // per_block, :, lane : lane + width] = tile.astype(BF16)


def attend(queries, keys, values, fresh_key, fresh_value, lengths, blocks):
    rows, heads, width = queries.shape
    vmem = pl.BlockSpec(memory_space=pltpu.VMEM)
    far = pl.BlockSpec(memory_space=pl.ANY)
    return pl.pallas_call(
        attend_kernel,
        name="attend",
        out_shape=jax.ShapeDtypeStruct((blocks, rows, heads * width // blocks), BF16),
        in_specs=[pl.BlockSpec(memory_space=pltpu.SMEM), vmem, far, far, vmem, vmem],
        out_specs=vmem,
        scratch_shapes=[
            pltpu.VMEM(keys.shape, BF16),
            pltpu.VMEM(values.shape, BF16),
            pltpu.VMEM(((rows + 1) * heads, width), F32),
            pltpu.SemaphoreType.DMA((rows // AT_ONCE,)),
            pltpu.SemaphoreType.DMA((rows // AT_ONCE,)),
        ],
        compiler_params=pltpu.CompilerParams(vmem_limit_bytes=FULL_VMEM),
        cost_estimate=pl.CostEstimate(
            flops=4 * keys.size * heads // keys.shape[1],
            bytes_accessed=4 * keys.size,
            transcendentals=0,
        ),
    )(lengths, queries, keys, values, fresh_key, fresh_value)


def whole(count):
    return [pl.BlockSpec(memory_space=pltpu.VMEM)] * count


TILES = 4


def project_kernel(order_ref, f_ref, w_hbm, own, ahead, back, ahead_last, back_last, *scratch):
    rows_ref, w_ref, out_ref, w_sem, o_sem = scratch
    block = f_ref.shape[1]
    tile = w_ref.shape[2]
    chunk = rows_ref.shape[0] // SIDE
    half = TILES // 2

    def arrival(k):
        return pltpu.make_async_copy(w_hbm.at[:, pl.ds(k * tile, tile)], w_ref.at[k], w_sem.at[k])

    def departure(k, part):
        low = k < half
        to = (
            own,
            ahead_last if low else ahead,
            ahead if low else back,
            back if low else back_last,
        )[part]
        column = (k if to.shape[1] == tile * TILES else k % half) * tile
        return pltpu.make_async_copy(
            out_ref.at[k, pl.ds(part * chunk, chunk)],
            to.at[:, pl.ds(column, tile)],
            o_sem.at[k, part],
        )

    for k in range(TILES):
        arrival(k).start()
    for k in range(SIDE * SIDE):
        rows_ref[k * block : (k + 1) * block, :] = f_ref[order_ref[k]]
    for k in range(TILES):
        arrival(k).wait()
        out_ref[k] = jnp.dot(rows_ref[...], w_ref[k], preferred_element_type=F32).astype(BF16)
        for part in range(SIDE):
            departure(k, part).start()
    for k in range(TILES):
        for part in range(SIDE):
            departure(k, part).wait()


def project(order, features, weight):
    blocks, rows, depth = features.shape
    cols = weight.shape[1]
    tile = cols // TILES
    chunk = blocks * rows // SIDE
    far = pl.BlockSpec(memory_space=pl.ANY)
    full = jax.ShapeDtypeStruct((chunk, cols), BF16)
    part = jax.ShapeDtypeStruct((chunk, cols // 2), BF16)
    return pl.pallas_call(
        project_kernel,
        name="project",
        out_shape=[full, full, full, part, part],
        in_specs=[
            pl.BlockSpec(memory_space=pltpu.SMEM),
            pl.BlockSpec(memory_space=pltpu.VMEM),
            far,
        ],
        out_specs=[far] * 5,
        scratch_shapes=[
            pltpu.VMEM((blocks * rows, depth), BF16),
            pltpu.VMEM((TILES, depth, tile), BF16),
            pltpu.VMEM((TILES, blocks * rows, tile), BF16),
            pltpu.SemaphoreType.DMA((TILES,)),
            pltpu.SemaphoreType.DMA((TILES, SIDE)),
        ],
        compiler_params=pltpu.CompilerParams(vmem_limit_bytes=56 * 1024 * 1024),
        cost_estimate=pl.CostEstimate(
            flops=2 * blocks * rows * depth * cols,
            bytes_accessed=2 * depth * cols + 2 * blocks * rows * cols,
            transcendentals=0,
        ),
    )(order, features, weight)


def meet_kernel(last, came, o_ref, *, first):
    came_half = came[:, first : first + o_ref.shape[1]]
    o_ref[...] = (last[...].astype(F32) + came_half.astype(F32)).astype(BF16)


def meet(last, came, first):
    return pl.pallas_call(
        lambda *refs: meet_kernel(*refs, first=first),
        name="meet",
        out_shape=jax.ShapeDtypeStruct(last.shape, BF16),
        in_specs=whole(2),
        out_specs=whole(1)[0],
        compiler_params=pltpu.CompilerParams(vmem_limit_bytes=VMEM_BYTES),
        cost_estimate=pl.CostEstimate(flops=2**20, bytes_accessed=2**22, transcendentals=0),
    )(last, came)


def join_kernel(own, came_ahead, came_back, ahead_last, back_last, *outs):
    rows = outs[0].shape[0]
    half = ahead_last.shape[1]
    for k in range(SIDE):
        at = slice(k * rows, (k + 1) * rows)
        for right in range(2):
            cols = slice(right * half, (right + 1) * half)
            total = own[at, cols].astype(F32)
            if right:
                total = total + came_ahead[at, cols].astype(F32) + back_last[at].astype(F32)
            else:
                total = total + ahead_last[at].astype(F32) + came_back[at, cols].astype(F32)
            outs[k][:, cols] = total.astype(BF16)


def join(*operands):
    rows, cols = operands[0].shape
    return pl.pallas_call(
        join_kernel,
        name="join",
        out_shape=[jax.ShapeDtypeStruct((rows // SIDE, cols), BF16)] * SIDE,
        in_specs=whole(5),
        out_specs=whole(SIDE),
        compiler_params=pltpu.CompilerParams(vmem_limit_bytes=VMEM_BYTES),
        cost_estimate=pl.CostEstimate(flops=2**20, bytes_accessed=2**22, transcendentals=0),
    )(*operands)


def dispatch_kernel(slot_ref, f_ref, _down, _up, *outs):
    count = outs[0].shape[0]
    rows = f_ref.shape[0]
    features = f_ref[...]
    for k in range(SIDE):
        slots = lax.broadcasted_iota(jnp.int32, (count, rows), 0) + k * count
        placing = (slots == slot_ref[...]).astype(F32).astype(BF16)
        outs[k][...] = jnp.dot(placing, features, preferred_element_type=F32).astype(BF16)


def dispatch(slot, features, count, down, up):
    rows, depth = features.shape
    return pl.pallas_call(
        dispatch_kernel,
        name="dispatch",
        out_shape=[jax.ShapeDtypeStruct((count, depth), BF16)] * SIDE,
        in_specs=whole(2) + [pl.BlockSpec(memory_space=pl.ANY)] * 2,
        out_specs=whole(SIDE),
        compiler_params=pltpu.CompilerParams(vmem_limit_bytes=VMEM_BYTES),
        cost_estimate=pl.CostEstimate(
            flops=2 * SIDE * count * rows * depth,
            bytes_accessed=2 * (rows + SIDE * count) * depth,
            transcendentals=0,
        ),
    )(slot, features, down, up)


QUAD = 4


def lanes_of(rows, rank, swapped):
    row = lax.broadcasted_iota(jnp.int32, (rows, 2 * rank), 0)
    lane = lax.broadcasted_iota(jnp.int32, (rows, 2 * rank), 1)
    member = (row % 16) // QUAD
    half = (lane // rank) ^ swapped
    return (member % 2) == half, member < 2


def shrink_kernel(s0, s1, s2, s3, own_ref, other_ref, o_ref):
    rank = o_ref.shape[1] // 2
    nt = (((1,), (1,)), ((), ()))
    quads = own_ref.shape[0] // (QUAD * rank)
    for pair in range(quads):
        total = None
        for swapped, weight_ref in ((0, own_ref), (1, other_ref)):
            quad = pair + swapped * quads
            rows = jnp.concatenate([s[quad * 16 : (quad + 1) * 16, :] for s in (s0, s1, s2, s3)])
            weight = weight_ref[pair * QUAD * rank : (pair + 1) * QUAD * rank, :]
            if swapped:
                weight = jnp.concatenate(
                    [weight[(m ^ 1) * rank : ((m ^ 1) + 1) * rank] for m in range(QUAD)]
                )
            got = lax.dot_general(rows, weight, nt, preferred_element_type=F32)
            mine, first = lanes_of(rows.shape[0], rank, swapped)
            kept = jnp.where(first, got[:, : 2 * rank], got[:, 2 * rank :])
            kept = jnp.where(mine, kept, 0.0)
            total = kept if total is None else total + kept
        o_ref[pair * 64 : (pair + 1) * 64, :] = total.astype(BF16)


def shrink(slots, own, other):
    rank = 64
    return pl.pallas_call(
        shrink_kernel,
        name="shrink",
        out_shape=jax.ShapeDtypeStruct((own.shape[0] // (QUAD * rank) * 64, 2 * rank), BF16),
        in_specs=whole(6),
        out_specs=whole(1)[0],
        compiler_params=pltpu.CompilerParams(vmem_limit_bytes=VMEM_BYTES),
        cost_estimate=pl.CostEstimate(flops=2**28, bytes_accessed=2**22, transcendentals=0),
    )(*slots, own, other)


def grow_kernel(h_ref, own_ref, other_ref, *outs):
    rank = h_ref.shape[1] // 2
    quads = own_ref.shape[0] // (QUAD * rank)
    for pair in range(quads):
        held = h_ref[pair * 64 : (pair + 1) * 64, :].astype(F32)
        for swapped, weight_ref in ((0, own_ref), (1, other_ref)):
            quad = pair + swapped * quads
            weight = weight_ref[pair * QUAD * rank : (pair + 1) * QUAD * rank, :]
            if swapped:
                weight = jnp.concatenate(
                    [weight[(m ^ 1) * rank : ((m ^ 1) + 1) * rank] for m in range(QUAD)]
                )
            mine, first = lanes_of(held.shape[0], rank, swapped)
            left = jnp.where(mine & first, held, 0.0).astype(BF16)
            right = jnp.where(mine & ~first, held, 0.0).astype(BF16)
            got = jnp.dot(
                jnp.concatenate([left, right], axis=1), weight, preferred_element_type=F32
            ).astype(BF16)
            for k in range(SIDE):
                outs[k][quad * 16 : (quad + 1) * 16, :] = got[k * 16 : (k + 1) * 16]


def grow(shrunk, own, other, count):
    return pl.pallas_call(
        grow_kernel,
        name="grow",
        out_shape=[jax.ShapeDtypeStruct((count, own.shape[1]), BF16)] * SIDE,
        in_specs=whole(3),
        out_specs=whole(SIDE),
        compiler_params=pltpu.CompilerParams(vmem_limit_bytes=VMEM_BYTES),
        cost_estimate=pl.CostEstimate(flops=2**28, bytes_accessed=2**22, transcendentals=0),
    )(shrunk, own, other)


def collect_kernel(slot_ref, r0, r1, r2, r3, o_ref):
    count = r0.shape[0]
    blocks, rows, cols = o_ref.shape
    total = jnp.zeros((blocks * rows, cols), F32)
    for k, ref in enumerate((r0, r1, r2, r3)):
        slots = lax.broadcasted_iota(jnp.int32, (count, blocks * rows), 0) + k * count
        placing = (slots == slot_ref[...]).astype(F32).astype(BF16)
        total = total + lax.dot_general(
            placing, ref[...], (((0,), (0,)), ((), ())), preferred_element_type=F32
        )
    for t in range(blocks):
        o_ref[t] = total[t * rows : (t + 1) * rows].astype(BF16)


def collect(slot, returned, blocks):
    rows = slot.shape[1]
    cols = returned[0].shape[1]
    return pl.pallas_call(
        collect_kernel,
        name="collect",
        out_shape=jax.ShapeDtypeStruct((blocks, rows // blocks, cols), BF16),
        in_specs=whole(5),
        out_specs=whole(1)[0],
        compiler_params=pltpu.CompilerParams(vmem_limit_bytes=VMEM_BYTES),
        cost_estimate=pl.CostEstimate(flops=2**28, bytes_accessed=2**21, transcendentals=0),
    )(slot, *returned)


def finish_kernel(skip_ref, s_ref, a_ref, b_ref, c_ref, delta_ref, o_ref):
    blocks, _, cols = delta_ref.shape
    for t in range(blocks):
        at = slice(t * cols, (t + 1) * cols)
        base = (
            s_ref[:, at].astype(F32)
            + a_ref[:, at].astype(F32)
            + b_ref[:, at].astype(F32)
            + c_ref[:, at].astype(F32)
        )
        o_ref[:, at] = (
            skip_ref[:, at].astype(F32) + base + 2.0 * delta_ref[t].astype(F32)
        ).astype(BF16)


def finish(*operands):
    rows_of = operands[0].shape
    return pl.pallas_call(
        finish_kernel,
        name="finish",
        out_shape=jax.ShapeDtypeStruct(operands[0].shape, BF16),
        grid=(1,),
        in_specs=[
            pl.BlockSpec(rows_of, lambda i: (0, 0)),
            pl.BlockSpec(rows_of, lambda i: (0, 0)),
            pl.BlockSpec(rows_of, lambda i: (0, 0)),
            pl.BlockSpec(rows_of, lambda i: (0, 0)),
            pl.BlockSpec(rows_of, lambda i: (0, 0)),
            pl.BlockSpec(operands[5].shape, lambda i: (0, 0, 0)),
        ],
        out_specs=pl.BlockSpec(rows_of, lambda i: (0, 0)),
        compiler_params=pltpu.CompilerParams(vmem_limit_bytes=VMEM_BYTES),
        cost_estimate=pl.CostEstimate(flops=2**20, bytes_accessed=2**21, transcendentals=0),
    )(*operands)


def wide_sum(*terms):
    return sum(term.astype(F32) for term in terms)


def body(
    queries,
    cached_key_rows,
    cached_value_rows,
    fresh_key,
    fresh_value,
    lengths,
    adapter_index,
    skip_stream,
    output_weight,
    adapter_down_weight,
    adapter_up_weight,
):
    blocks = lax.axis_size("tp")
    rep, tp = lax.axis_index("rep"), lax.axis_index("tp")
    held, depth, rank = adapter_down_weight.shape
    width = output_weight.shape[1]

    down_own = jnp.swapaxes(adapter_down_weight, 1, 2).reshape(held * rank, depth)
    up_own = adapter_up_weight.reshape(held * rank, depth)
    down_other = pass_core(down_own)
    up_other = pass_core(up_own)

    adapter = adapter_index[:, 0]
    rows = adapter.shape[0]
    same = adapter[:, None] == adapter[None, :]
    count_up = jnp.arange(rows, dtype=jnp.int32)
    ranked = jnp.sum((same & (count_up[:, None] > count_up[None, :])).astype(jnp.int32), axis=1)
    owner = adapter // held
    cap = 4
    per_z = 2 * held * cap
    slot = (
        (owner // 2 - rep // 2) % SIDE * per_z
        + ((owner % 2) ^ (rep % 2)) * (held * cap)
        + (adapter % held) * cap
        + ranked
    ).reshape(1, rows)
    order = lax.dynamic_slice(jnp.asarray(row_order()), (rep * blocks + tp, 0), (1, blocks))[0]

    attended = attend(
        queries, cached_key_rows, cached_value_rows, fresh_key, fresh_value, lengths, blocks
    )
    features = lax.all_to_all(attended, "tp", split_axis=0, concat_axis=0, tiled=True)
    flat = features.reshape(rows, depth)

    placed = dispatch(slot, flat, per_z, down_other, up_other)
    arrived = [placed[0]] + [pass_z(placed[k], k) for k in range(1, SIDE)]

    own, ahead, back, ahead_last, back_last = project(order, features, output_weight)
    ahead, *arrived = lax.optimization_barrier((ahead, *arrived))
    came_ahead, came_back = pass_plane(ahead, "xy", 1), pass_plane(back, "xy", -1)

    shrunk = shrink(arrived, down_own, down_other)
    near = [pass_plane(shrunk, "yx", k) for k in range(1, SIDE)]
    shrunk = wide_sum(shrunk, *near).astype(BF16)
    near = [pass_plane(shrunk, "xy", k) for k in range(1, SIDE)]
    back_last = meet(back_last, came_back, back_last.shape[1])
    ahead_last = meet(ahead_last, came_ahead, 0)
    *near, ahead_last = lax.optimization_barrier((*near, ahead_last))
    shrunk = wide_sum(shrunk, *near).astype(BF16)
    ahead_last, back_last = pass_plane(ahead_last, "xy", 1), pass_plane(back_last, "xy", -1)
    grown = grow(shrunk, up_own, up_other, per_z)
    returned = [grown[0]] + [pass_z(grown[k], -k) for k in range(1, SIDE)]
    returned[1], returned[2], back_last = lax.optimization_barrier((returned[1], returned[2], back_last))
    summed = join(own, came_ahead, came_back, ahead_last, back_last)
    delta = collect(slot, returned, blocks)

    second = [pass_plane(summed[k], "yx", k) for k in range(1, SIDE)]
    delta = lax.all_to_all(delta, "tp", split_axis=0, concat_axis=0, tiled=True)
    return finish(skip_stream, summed[0], *second, delta)


def solution(mesh):
    return jax.shard_map(
        body,
        mesh=mesh,
        in_specs=(
            P(BOTH, None, None),
            P(BOTH, None, None, None),
            P(BOTH, None, None, None),
            P(BOTH, None, None),
            P(BOTH, None, None),
            P(BOTH),
            P("rep", None),
            P(BOTH, None),
            P("tp", None),
            P("rep", "tp", None),
            P("rep", None, "tp"),
        ),
        out_specs=P(BOTH, None),
        check_vma=False,
    )
```

```python
import math

import jax
import jax.numpy as jnp
import numpy as np
from jax import lax
from jax.experimental import pallas as pl
from jax.experimental.pallas import tpu as pltpu
from jax.sharding import PartitionSpec as P

F32 = jnp.float32
BF16 = jnp.bfloat16
BOTH = ("rep", "tp")
SIDE = 4
VMEM_BYTES = 24 * 1024 * 1024
FULL_VMEM = 60 * 1024 * 1024


def place(z, c, y, x):
    return ((z * 2 + c) * SIDE + y) * SIDE + x


PLACES = [
    (z, c, y, x) for z in range(SIDE) for c in range(2) for y in range(SIDE) for x in range(SIDE)
]


def pass_plane(value, axis_of_core, offset):
    pairs = []
    for z, c, y, x in PLACES:
        if axis_of_core[c] == "x":
            to = place(z, c, y, (x + offset) % SIDE)
        else:
            to = place(z, c, (y + offset) % SIDE, x)
        pairs.append((place(z, c, y, x), to))
    return lax.ppermute(value, BOTH, pairs)


def pass_z(value, offset):
    pairs = [(place(z, c, y, x), place((z + offset) % SIDE, c, y, x)) for z, c, y, x in PLACES]
    return lax.ppermute(value, BOTH, pairs)


def pass_core(value):
    return lax.ppermute(
        value, BOTH, [(place(z, c, y, x), place(z, 1 - c, y, x)) for z, c, y, x in PLACES]
    )


def row_order():
    table = np.zeros((len(PLACES), SIDE * SIDE), np.int32)
    for z, c, y, x in PLACES:
        for first in range(SIDE):
            for second in range(SIDE):
                dx, dy = (first, second) if c == 0 else (second, first)
                table[place(z, c, y, x), first * SIDE + second] = (
                    (y + dy) % SIDE * SIDE + (x + dx) % SIDE
                )
    return table


AT_ONCE = 8


def attend_kernel(
    lengths_ref, q_ref, k_hbm, v_hbm, fk_ref, fv_ref, o_ref, k_ref, v_ref, mixed_ref, k_sem, v_sem
):
    rows, heads, width = q_ref.shape
    groups, span = k_ref.shape[1], k_ref.shape[2]
    fold = heads // groups
    steps = rows // AT_ONCE
    factor = 1.0 / math.sqrt(width)
    nt = (((1,), (1,)), ((), ()))

    def copy(step, far, near, sem):
        at = pl.ds(step * AT_ONCE, AT_ONCE)
        return pltpu.make_async_copy(far.at[at], near.at[at], sem.at[step])

    for step in range(steps):
        copy(step, k_hbm, k_ref, k_sem).start()
        copy(step, v_hbm, v_ref, v_sem).start()

    def one_step(step, carry):
        copy(step, k_hbm, k_ref, k_sem).wait()

        all_scores = []
        for item in range(AT_ONCE):
            row = step * AT_ONCE + item
            q = q_ref[row]
            parts = []
            for g in range(groups):
                two = q[(g // 2) * 2 * fold : (g // 2 + 1) * 2 * fold]
                got = lax.dot_general(two, k_ref[row, g], nt, preferred_element_type=F32)
                parts.append(got[(g % 2) * fold : (g % 2 + 1) * fold])
            all_scores.append(jnp.concatenate(parts, axis=0) * factor)
        copy(step, v_hbm, v_ref, v_sem).wait()
        for item in range(AT_ONCE):
            row = step * AT_ONCE + item
            scores = all_scores[item]
            fresh_k = jnp.broadcast_to(
                fk_ref[row].astype(F32)[:, None, :], (groups, fold, width)
            ).reshape(heads, width)
            own = jnp.sum(q_ref[row].astype(F32) * fresh_k, axis=-1, keepdims=True) * factor
            position = lax.broadcasted_iota(jnp.int32, (heads, span), 1)
            masked = jnp.where(position < lengths_ref[row], scores, -jnp.inf)
            top = jnp.maximum(jnp.max(masked, axis=-1, keepdims=True), own)
            expo = jnp.exp(masked - top)
            expo_own = jnp.exp(own - top)
            inverse = 1.0 / (jnp.sum(expo, axis=-1, keepdims=True) + expo_own)
            probs = (expo * inverse).astype(BF16)
            probs_own = (expo_own * inverse).astype(BF16).astype(F32)
            parts = []
            for g in range(groups):
                two = probs[(g // 2) * 2 * fold : (g // 2 + 1) * 2 * fold]
                got = jnp.dot(two, v_ref[row, g], preferred_element_type=F32)
                parts.append(got[(g % 2) * fold : (g % 2 + 1) * fold])
            fresh_v = jnp.broadcast_to(
                fv_ref[row].astype(F32)[:, None, :], (groups, fold, width)
            ).reshape(heads, width)
            mixed = jnp.concatenate(parts, axis=0) + probs_own * fresh_v
            mixed_ref[pl.ds(pl.multiple_of(row * heads, heads), heads), :] = mixed
        return carry

    lax.fori_loop(0, steps, one_step, 0)
    per_block = o_ref.shape[2] // width
    for h in range(heads):
        tile = jnp.concatenate(
            [
                mixed_ref[pl.ds(half * 8 * heads + h, 8, stride=heads), :]
                for half in range(rows // 8)
            ],
            axis=0,
        )
        lane = (h % per_block) * width
        o_ref[h // per_block, :, lane : lane + width] = tile.astype(BF16)


def attend(queries, keys, values, fresh_key, fresh_value, lengths, blocks):
    rows, heads, width = queries.shape
    vmem = pl.BlockSpec(memory_space=pltpu.VMEM)
    far = pl.BlockSpec(memory_space=pl.ANY)
    return pl.pallas_call(
        attend_kernel,
        name="attend",
        out_shape=jax.ShapeDtypeStruct((blocks, rows, heads * width // blocks), BF16),
        in_specs=[pl.BlockSpec(memory_space=pltpu.SMEM), vmem, far, far, vmem, vmem],
        out_specs=vmem,
        scratch_shapes=[
            pltpu.VMEM(keys.shape, BF16),
            pltpu.VMEM(values.shape, BF16),
            pltpu.VMEM(((rows + 1) * heads, width), F32),
            pltpu.SemaphoreType.DMA((rows // AT_ONCE,)),
            pltpu.SemaphoreType.DMA((rows // AT_ONCE,)),
        ],
        compiler_params=pltpu.CompilerParams(vmem_limit_bytes=FULL_VMEM),
        cost_estimate=pl.CostEstimate(
            flops=4 * keys.size * heads // keys.shape[1],
            bytes_accessed=4 * keys.size,
            transcendentals=0,
        ),
    )(lengths, queries, keys, values, fresh_key, fresh_value)


def whole(count):
    return [pl.BlockSpec(memory_space=pltpu.VMEM)] * count


TILES = 4


def project_kernel(order_ref, f_ref, w_hbm, own, ahead, back, ahead_last, back_last, *scratch):
    rows_ref, w_ref, out_ref, w_sem, o_sem = scratch
    block = f_ref.shape[1]
    tile = w_ref.shape[2]
    chunk = rows_ref.shape[0] // SIDE
    half = TILES // 2

    def arrival(k):
        return pltpu.make_async_copy(w_hbm.at[:, pl.ds(k * tile, tile)], w_ref.at[k], w_sem.at[k])

    def departure(k, part):
        low = k < half
        to = (
            own,
            ahead_last if low else ahead,
            ahead if low else back,
            back if low else back_last,
        )[part]
        column = (k if to.shape[1] == tile * TILES else k % half) * tile
        return pltpu.make_async_copy(
            out_ref.at[k, pl.ds(part * chunk, chunk)],
            to.at[:, pl.ds(column, tile)],
            o_sem.at[k, part],
        )

    for k in range(TILES):
        arrival(k).start()
    for k in range(SIDE * SIDE):
        rows_ref[k * block : (k + 1) * block, :] = f_ref[order_ref[k]]
    for k in range(TILES):
        arrival(k).wait()
        out_ref[k] = jnp.dot(rows_ref[...], w_ref[k], preferred_element_type=F32).astype(BF16)
        for part in range(SIDE):
            departure(k, part).start()
    for k in range(TILES):
        for part in range(SIDE):
            departure(k, part).wait()


def project(order, features, weight):
    blocks, rows, depth = features.shape
    cols = weight.shape[1]
    tile = cols // TILES
    chunk = blocks * rows // SIDE
    far = pl.BlockSpec(memory_space=pl.ANY)
    full = jax.ShapeDtypeStruct((chunk, cols), BF16)
    part = jax.ShapeDtypeStruct((chunk, cols // 2), BF16)
    return pl.pallas_call(
        project_kernel,
        name="project",
        out_shape=[full, full, full, part, part],
        in_specs=[
            pl.BlockSpec(memory_space=pltpu.SMEM),
            pl.BlockSpec(memory_space=pltpu.VMEM),
            far,
        ],
        out_specs=[far] * 5,
        scratch_shapes=[
            pltpu.VMEM((blocks * rows, depth), BF16),
            pltpu.VMEM((TILES, depth, tile), BF16),
            pltpu.VMEM((TILES, blocks * rows, tile), BF16),
            pltpu.SemaphoreType.DMA((TILES,)),
            pltpu.SemaphoreType.DMA((TILES, SIDE)),
        ],
        compiler_params=pltpu.CompilerParams(vmem_limit_bytes=56 * 1024 * 1024),
        cost_estimate=pl.CostEstimate(
            flops=2 * blocks * rows * depth * cols,
            bytes_accessed=2 * depth * cols + 2 * blocks * rows * cols,
            transcendentals=0,
        ),
    )(order, features, weight)


def meet_kernel(last, came, o_ref, *, first):
    came_half = came[:, first : first + o_ref.shape[1]]
    o_ref[...] = (last[...].astype(F32) + came_half.astype(F32)).astype(BF16)


def meet(last, came, first):
    return pl.pallas_call(
        lambda *refs: meet_kernel(*refs, first=first),
        name="meet",
        out_shape=jax.ShapeDtypeStruct(last.shape, BF16),
        in_specs=whole(2),
        out_specs=whole(1)[0],
        compiler_params=pltpu.CompilerParams(vmem_limit_bytes=VMEM_BYTES),
        cost_estimate=pl.CostEstimate(flops=2**20, bytes_accessed=2**22, transcendentals=0),
    )(last, came)


def join_kernel(own, came_ahead, came_back, ahead_last, back_last, *outs):
    rows = outs[0].shape[0]
    half = ahead_last.shape[1]
    for k in range(SIDE):
        at = slice(k * rows, (k + 1) * rows)
        for right in range(2):
            cols = slice(right * half, (right + 1) * half)
            total = own[at, cols].astype(F32)
            if right:
                total = total + came_ahead[at, cols].astype(F32) + back_last[at].astype(F32)
            else:
                total = total + ahead_last[at].astype(F32) + came_back[at, cols].astype(F32)
            outs[k][:, cols] = total.astype(BF16)


def join(*operands):
    rows, cols = operands[0].shape
    return pl.pallas_call(
        join_kernel,
        name="join",
        out_shape=[jax.ShapeDtypeStruct((rows // SIDE, cols), BF16)] * SIDE,
        in_specs=whole(5),
        out_specs=whole(SIDE),
        compiler_params=pltpu.CompilerParams(vmem_limit_bytes=VMEM_BYTES),
        cost_estimate=pl.CostEstimate(flops=2**20, bytes_accessed=2**22, transcendentals=0),
    )(*operands)


def dispatch_kernel(slot_ref, f_ref, _down, _up, *outs):
    count = outs[0].shape[0]
    rows = f_ref.shape[0]
    features = f_ref[...]
    for k in range(SIDE):
        slots = lax.broadcasted_iota(jnp.int32, (count, rows), 0) + k * count
        placing = (slots == slot_ref[...]).astype(F32).astype(BF16)
        outs[k][...] = jnp.dot(placing, features, preferred_element_type=F32).astype(BF16)


def dispatch(slot, features, count, down, up):
    rows, depth = features.shape
    return pl.pallas_call(
        dispatch_kernel,
        name="dispatch",
        out_shape=[jax.ShapeDtypeStruct((count, depth), BF16)] * SIDE,
        in_specs=whole(2) + [pl.BlockSpec(memory_space=pl.ANY)] * 2,
        out_specs=whole(SIDE),
        compiler_params=pltpu.CompilerParams(vmem_limit_bytes=VMEM_BYTES),
        cost_estimate=pl.CostEstimate(
            flops=2 * SIDE * count * rows * depth,
            bytes_accessed=2 * (rows + SIDE * count) * depth,
            transcendentals=0,
        ),
    )(slot, features, down, up)


QUAD = 4


def lanes_of(rows, rank, swapped):
    row = lax.broadcasted_iota(jnp.int32, (rows, 2 * rank), 0)
    lane = lax.broadcasted_iota(jnp.int32, (rows, 2 * rank), 1)
    member = (row % 16) // QUAD
    half = (lane // rank) ^ swapped
    return (member % 2) == half, member < 2


def shrink_kernel(s0, s1, s2, s3, own_ref, other_ref, o_ref):
    rank = o_ref.shape[1] // 2
    nt = (((1,), (1,)), ((), ()))
    quads = own_ref.shape[0] // (QUAD * rank)
    for pair in range(quads):
        total = None
        for swapped, weight_ref in ((0, own_ref), (1, other_ref)):
            quad = pair + swapped * quads
            rows = jnp.concatenate([s[quad * 16 : (quad + 1) * 16, :] for s in (s0, s1, s2, s3)])
            weight = weight_ref[pair * QUAD * rank : (pair + 1) * QUAD * rank, :]
            if swapped:
                weight = jnp.concatenate(
                    [weight[(m ^ 1) * rank : ((m ^ 1) + 1) * rank] for m in range(QUAD)]
                )
            got = lax.dot_general(rows, weight, nt, preferred_element_type=F32)
            mine, first = lanes_of(rows.shape[0], rank, swapped)
            kept = jnp.where(first, got[:, : 2 * rank], got[:, 2 * rank :])
            kept = jnp.where(mine, kept, 0.0)
            total = kept if total is None else total + kept
        o_ref[pair * 64 : (pair + 1) * 64, :] = total.astype(BF16)


def shrink(slots, own, other):
    rank = 64
    return pl.pallas_call(
        shrink_kernel,
        name="shrink",
        out_shape=jax.ShapeDtypeStruct((own.shape[0] // (QUAD * rank) * 64, 2 * rank), BF16),
        in_specs=whole(6),
        out_specs=whole(1)[0],
        compiler_params=pltpu.CompilerParams(vmem_limit_bytes=VMEM_BYTES),
        cost_estimate=pl.CostEstimate(flops=2**28, bytes_accessed=2**22, transcendentals=0),
    )(*slots, own, other)


def grow_kernel(h_ref, own_ref, other_ref, *outs):
    rank = h_ref.shape[1] // 2
    quads = own_ref.shape[0] // (QUAD * rank)
    for pair in range(quads):
        held = h_ref[pair * 64 : (pair + 1) * 64, :].astype(F32)
        for swapped, weight_ref in ((0, own_ref), (1, other_ref)):
            quad = pair + swapped * quads
            weight = weight_ref[pair * QUAD * rank : (pair + 1) * QUAD * rank, :]
            if swapped:
                weight = jnp.concatenate(
                    [weight[(m ^ 1) * rank : ((m ^ 1) + 1) * rank] for m in range(QUAD)]
                )
            mine, first = lanes_of(held.shape[0], rank, swapped)
            left = jnp.where(mine & first, held, 0.0).astype(BF16)
            right = jnp.where(mine & ~first, held, 0.0).astype(BF16)
            got = jnp.dot(
                jnp.concatenate([left, right], axis=1), weight, preferred_element_type=F32
            ).astype(BF16)
            for k in range(SIDE):
                outs[k][quad * 16 : (quad + 1) * 16, :] = got[k * 16 : (k + 1) * 16]


def grow(shrunk, own, other, count):
    return pl.pallas_call(
        grow_kernel,
        name="grow",
        out_shape=[jax.ShapeDtypeStruct((count, own.shape[1]), BF16)] * SIDE,
        in_specs=whole(3),
        out_specs=whole(SIDE),
        compiler_params=pltpu.CompilerParams(vmem_limit_bytes=VMEM_BYTES),
        cost_estimate=pl.CostEstimate(flops=2**28, bytes_accessed=2**22, transcendentals=0),
    )(shrunk, own, other)


def collect_kernel(slot_ref, r0, r1, r2, r3, o_ref):
    count = r0.shape[0]
    blocks, rows, cols = o_ref.shape
    total = jnp.zeros((blocks * rows, cols), F32)
    for k, ref in enumerate((r0, r1, r2, r3)):
        slots = lax.broadcasted_iota(jnp.int32, (count, blocks * rows), 0) + k * count
        placing = (slots == slot_ref[...]).astype(F32).astype(BF16)
        total = total + lax.dot_general(
            placing, ref[...], (((0,), (0,)), ((), ())), preferred_element_type=F32
        )
    for t in range(blocks):
        o_ref[t] = total[t * rows : (t + 1) * rows].astype(BF16)


def collect(slot, returned, blocks):
    rows = slot.shape[1]
    cols = returned[0].shape[1]
    return pl.pallas_call(
        collect_kernel,
        name="collect",
        out_shape=jax.ShapeDtypeStruct((blocks, rows // blocks, cols), BF16),
        in_specs=whole(5),
        out_specs=whole(1)[0],
        compiler_params=pltpu.CompilerParams(vmem_limit_bytes=VMEM_BYTES),
        cost_estimate=pl.CostEstimate(flops=2**28, bytes_accessed=2**21, transcendentals=0),
    )(slot, *returned)


def finish_kernel(skip_ref, s_ref, a_ref, b_ref, c_ref, delta_ref, o_ref):
    blocks, _, cols = delta_ref.shape
    for t in range(blocks):
        at = slice(t * cols, (t + 1) * cols)
        base = (
            s_ref[:, at].astype(F32)
            + a_ref[:, at].astype(F32)
            + b_ref[:, at].astype(F32)
            + c_ref[:, at].astype(F32)
        )
        o_ref[:, at] = (
            skip_ref[:, at].astype(F32) + base + 2.0 * delta_ref[t].astype(F32)
        ).astype(BF16)


def finish(*operands):
    rows_of = operands[0].shape
    return pl.pallas_call(
        finish_kernel,
        name="finish",
        out_shape=jax.ShapeDtypeStruct(operands[0].shape, BF16),
        grid=(1,),
        in_specs=[
            pl.BlockSpec(rows_of, lambda i: (0, 0)),
            pl.BlockSpec(rows_of, lambda i: (0, 0)),
            pl.BlockSpec(rows_of, lambda i: (0, 0)),
            pl.BlockSpec(rows_of, lambda i: (0, 0)),
            pl.BlockSpec(rows_of, lambda i: (0, 0)),
            pl.BlockSpec(operands[5].shape, lambda i: (0, 0, 0)),
        ],
        out_specs=pl.BlockSpec(rows_of, lambda i: (0, 0)),
        compiler_params=pltpu.CompilerParams(vmem_limit_bytes=VMEM_BYTES),
        cost_estimate=pl.CostEstimate(flops=2**20, bytes_accessed=2**21, transcendentals=0),
    )(*operands)


def wide_sum(*terms):
    return sum(term.astype(F32) for term in terms)


def body(
    queries,
    cached_key_rows,
    cached_value_rows,
    fresh_key,
    fresh_value,
    lengths,
    adapter_index,
    skip_stream,
    output_weight,
    adapter_down_weight,
    adapter_up_weight,
):
    blocks = lax.axis_size("tp")
    rep, tp = lax.axis_index("rep"), lax.axis_index("tp")
    held, depth, rank = adapter_down_weight.shape
    width = output_weight.shape[1]

    down_own = jnp.swapaxes(adapter_down_weight, 1, 2).reshape(held * rank, depth)
    up_own = adapter_up_weight.reshape(held * rank, depth)
    down_other = pass_core(down_own)
    up_other = pass_core(up_own)

    adapter = adapter_index[:, 0]
    rows = adapter.shape[0]
    same = adapter[:, None] == adapter[None, :]
    count_up = jnp.arange(rows, dtype=jnp.int32)
    ranked = jnp.sum((same & (count_up[:, None] > count_up[None, :])).astype(jnp.int32), axis=1)
    owner = adapter // held
    cap = 4
    per_z = 2 * held * cap
    slot = (
        (owner // 2 - rep // 2) % SIDE * per_z
        + ((owner % 2) ^ (rep % 2)) * (held * cap)
        + (adapter % held) * cap
        + ranked
    ).reshape(1, rows)
    order = lax.dynamic_slice(jnp.asarray(row_order()), (rep * blocks + tp, 0), (1, blocks))[0]

    attended = attend(
        queries, cached_key_rows, cached_value_rows, fresh_key, fresh_value, lengths, blocks
    )
    features = lax.all_to_all(attended, "tp", split_axis=0, concat_axis=0, tiled=True)
    flat = features.reshape(rows, depth)

    placed = dispatch(slot, flat, per_z, down_other, up_other)
    arrived = [placed[0]] + [pass_z(placed[k], k) for k in range(1, SIDE)]

    own, ahead, back, ahead_last, back_last = project(order, features, output_weight)
    ahead, *arrived = lax.optimization_barrier((ahead, *arrived))
    came_ahead, came_back = pass_plane(ahead, "xy", 1), pass_plane(back, "xy", -1)

    shrunk = shrink(arrived, down_own, down_other)
    near = [pass_plane(shrunk, "yx", k) for k in range(1, SIDE)]
    shrunk = wide_sum(shrunk, *near).astype(BF16)
    near = [pass_plane(shrunk, "xy", k) for k in range(1, SIDE)]
    back_last = meet(back_last, came_back, back_last.shape[1])
    ahead_last = meet(ahead_last, came_ahead, 0)
    *near, ahead_last = lax.optimization_barrier((*near, ahead_last))
    shrunk = wide_sum(shrunk, *near).astype(BF16)
    ahead_last, back_last = pass_plane(ahead_last, "xy", 1), pass_plane(back_last, "xy", -1)
    grown = grow(shrunk, up_own, up_other, per_z)
    returned = [grown[0]] + [pass_z(grown[k], -k) for k in range(1, SIDE)]
    returned[1], returned[2], back_last = lax.optimization_barrier((returned[1], returned[2], back_last))
    summed = join(own, came_ahead, came_back, ahead_last, back_last)
    delta = collect(slot, returned, blocks)

    second = [pass_plane(summed[k], "yx", k) for k in range(1, SIDE)]
    delta = lax.all_to_all(delta, "tp", split_axis=0, concat_axis=0, tiled=True)
    return finish(skip_stream, summed[0], *second, delta)


def solution(mesh):
    return jax.shard_map(
        body,
        mesh=mesh,
        in_specs=(
            P(BOTH, None, None),
            P(BOTH, None, None, None),
            P(BOTH, None, None, None),
            P(BOTH, None, None),
            P(BOTH, None, None),
            P(BOTH),
            P("rep", None),
            P(BOTH, None),
            P("tp", None),
            P("rep", "tp", None),
            P("rep", None, "tp"),
        ),
        out_specs=P(BOTH, None),
        check_vma=False,
    )
```
